512 devices in a mesh: prow: 32 (over y, x), pcol: 16 (over z, core).
Axes of the slice: x: 4, y: 8, z: 8, core: 2. Of those that a mesh axis runs over, the one named last changes fastest.
Arguments:
- direction: float32 [3, 4096, 4096], P(None, 'prow', 'pcol'), may hold values from -6 to 6
- state: float32 [3, 4096, 4096], P(None, 'prow', 'pcol'), may hold values from -4 to 4
- material: int32 [4096, 4096], P('prow', 'pcol'), may hold values from 0 to 7
- trimmed: int32 [4096, 4096], P('prow', 'pcol'), may hold values 0 or 1
- moduli: float32 [8], replicated, may hold values from 0.5 to 4
- band: int32 [32, 16], P('prow', 'pcol'), may hold values from 64 to 256
- blocks: bfloat16 [32, 16, 3, 256, 256], P('prow', 'pcol')
- basis: bfloat16 [16, 4096, 4096], P(None, 'prow', 'pcol'), may hold values from -0.03125 to 0.03125
- coarse_inverse: float32 [48, 48], replicated
Outputs:
- product: float32 [3, 4096, 4096], P(None, 'prow', 'pcol')
The draws below stay inside these ranges and needn't reach their ends.
All inputs are finite; a program needn't handle non-finite values. No bound on the sum of `trimmed` on one device may be relied on, other than what follows from the above.
Results may differ from the reference program's by a relative error of at most 0.0036.
Values may be sent and summed in bfloat16 or wider, within the bound.
A program may use at most 64 MiB of HBM per device.

```python
import math
import jax
import jax.numpy as jnp
from jax import lax

CX = 128
CY = 256
NCO = 16
NMAT = 8
H = 64
XB = 256
NX = 4096
NY = 4096
N_PROW = 32
N_PCOL = 16


def dominant(key, shape, width, lo, hi):
    first, second = jax.random.split(key)
    diag = jax.random.uniform(first, shape[:-1], jnp.float32, lo, hi)
    noise = jax.random.normal(second, shape, jnp.float32)
    eye = (jnp.arange(width)[:, None] == jnp.arange(width)[None, :]).astype(jnp.float32)
    off = noise * (0.6 / width ** 0.5) * diag[..., None]
    return eye * diag[..., None] + (1.0 - eye) * off


def draw_blocks(key, part):
    key = jax.random.fold_in(key, 11)
    shape = (N_PROW, N_PCOL, 3, XB, XB)
    return dominant(key, shape, XB, 0.04, 0.16).astype(jnp.bfloat16)


def draw_coarse_inverse(key, part):
    key = jax.random.fold_in(key, 23)
    width = 3 * NCO
    scale = 1.0 / width ** 0.5
    return dominant(key, (width, width), width, scale, 2.0 * scale)


def plant(values, stream_key, low, high):
    longest = values.shape.index(max(values.shape))
    spots = []
    for shift in (0, 1):
        where = [jax.random.randint(jax.random.fold_in(stream_key, axis), (), 0, length) for axis, length in enumerate(values.shape)]
        where[longest] = (where[longest] + shift) % values.shape[longest]
        spots.append(tuple(where))
    return values.at[spots[0]].set(low).at[spots[1]].set(high)


def levels(stream_key, dims, cuts, least, largest):
    factor_of = 1.0
    for dim, parts in cuts:
        draws = jax.random.uniform(jax.random.fold_in(jax.random.fold_in(stream_key, 6), dim), (parts,), jnp.float32, least / len(cuts), largest / len(cuts))
        factor_of = factor_of * jnp.repeat(jnp.exp(draws), dims[dim] // parts).reshape((-1,) + (1,) * (len(dims) - 1 - dim))
    return factor_of


def normal_values(rng, extent, scale, most, shards=(), kind=jnp.bfloat16):
    result = jax.random.normal(rng, extent, jnp.float32) * scale
    if len(shards) > 0:
        result = levels(rng, extent, shards, -0.22, 0.18) * result
    return jnp.clip(result, min=-most, max=most).astype(kind)


def setup_inputs(seed: int = 0) -> dict:
    seeds = jax.random.split(jax.random.key(seed), 10)
    return {
        "direction": normal_values(seeds[0], (3, NX, NY), 1.0, 6.0, ((1, 32), (2, 16)), jnp.float32),
        "state": normal_values(seeds[1], (3, NX, NY), 1.0, 4.0, ((1, 32), (2, 16)), jnp.float32),
        "material": plant(jax.random.randint(seeds[2], (NX, NY), 0, NMAT), jax.random.fold_in(seeds[2], 1), 0, NMAT - 1).astype(jnp.int32),
        "trimmed": plant((jax.random.randint(seeds[3], (NX, NY), 0, 4) < 3).astype(jnp.int32), jax.random.fold_in(seeds[3], 1), 0, 1),
        "moduli": jnp.clip(jnp.exp(jax.random.uniform(seeds[4], (NMAT,), jnp.float32, math.log(0.5), math.log(4.0))), 0.5, 4.0),
        "band": plant(jax.random.randint(seeds[5], (N_PROW, N_PCOL), XB // 4, XB + 1), jax.random.fold_in(seeds[5], 1), XB // 4, XB).astype(jnp.int32),
        "blocks": draw_blocks(jax.random.fold_in(seeds[9], 71), 0),
        "basis": normal_values(seeds[7], (NCO, NX, NY), (CX * CY) ** -0.5, 0.03125, ((1, 32), (2, 16))),
        "coarse_inverse": draw_coarse_inverse(jax.random.fold_in(seeds[9], 71), 0),
    }


def coefficients(state, material, trimmed, moduli):
    stretch = 1.0 + 0.3 * jnp.sum(state * state, axis=0)
    table = jnp.zeros(material.shape, jnp.float32)
    for entry in range(NMAT):
        table = table + jnp.where(material == entry, moduli[entry], jnp.float32(0.0))
    return table * (stretch + 1.0 / stretch) * (0.25 + 0.75 * trimmed.astype(jnp.float32))


def tangent(padded, coef):
    centre = padded[:, 1:-1, 1:-1]
    beside = padded[:, 2:, 1:-1] + padded[:, :-2, 1:-1] + padded[:, 1:-1, 2:] + padded[:, 1:-1, :-2]
    coupled = jnp.roll(centre, -1, axis=0)
    return coef * (5.0 * centre - beside + 0.5 * coupled)


def reference(direction, state, material, trimmed, moduli, band, blocks, basis, coarse_inverse):
    coef = coefficients(state, material, trimmed, moduli)
    tang = tangent(jnp.pad(direction, ((0, 0), (1, 1), (1, 1))), coef).astype(jnp.bfloat16)
    wide = jnp.pad(tang, ((0, 0), (H, H), (0, 0)))
    span = jnp.arange(XB, dtype=jnp.int32)
    dist = jnp.abs(span[:, None] - span[None, :])
    omega = jnp.where((span < H) | (span >= H + CX), 0.5, 1.0).astype(jnp.float32)

    def one(index, total):
        start = (index * CX).astype(jnp.int32)
        rows = lax.dynamic_slice_in_dim(wide, start, XB, 1).astype(jnp.float32)
        rows = rows.reshape(3, XB, N_PCOL, CY)
        mats = lax.dynamic_index_in_dim(blocks, index, 0, keepdims=False)
        widths = lax.dynamic_index_in_dim(band, index, 0, keepdims=False)
        mats = jnp.where(dist[None, None] <= widths[:, None, None, None], mats, jnp.zeros_like(mats))
        local = jnp.einsum('ects,csej->ctej', mats.astype(jnp.float32), rows)
        local = (local * omega[None, :, None, None]).reshape(3, XB, NY)
        window = lax.dynamic_slice_in_dim(total, start, XB, 1)
        return lax.dynamic_update_slice_in_dim(total, window + local, start, 1)

    total = lax.fori_loop(jnp.int32(0), jnp.int32(N_PROW), one, jnp.zeros((3, NX + 2 * H, NY), jnp.float32))
    assembled = total[:, H:H + NX, :]
    flat_basis = basis.reshape(NCO, NX * NY)
    coarse_sum = jnp.einsum('cp,kp->ck', tang.reshape(3, NX * NY).astype(jnp.float32), flat_basis.astype(jnp.float32))
    coarse_step = jnp.dot(coarse_inverse, coarse_sum.reshape(3 * NCO), precision=lax.Precision.HIGHEST)
    coarse_step = coarse_step.reshape(3, NCO).astype(jnp.bfloat16)
    coarse_term = jnp.dot(coarse_step, flat_basis, preferred_element_type=jnp.float32).reshape(3, NX, NY)
    return assembled + coarse_term
```

```python
import functools

import jax
import jax.numpy as jnp
from jax import lax
from jax.experimental import pallas as pl
from jax.experimental.pallas import tpu as pltpu
from jax.sharding import PartitionSpec as P

MESH = pl.DeviceIdType.MESH
F32 = jnp.float32
BF16 = jnp.bfloat16
NT = (((1,), (1,)), ((), ()))
TN = (((0,), (0,)), ((), ()))


def iota(shape, dim):
    return lax.broadcasted_iota(jnp.int32, shape, dim)


def mm(a, b, dims=(((1,), (0,)), ((), ()))):
    return lax.dot_general(a, b, dims, preferred_element_type=F32)


def ones_where(cond):
    return jnp.where(cond, 1.0, 0.0).astype(BF16)


def kernel(
    nrow,
    ncol,
    dir_hbm,
    state_hbm,
    mat_hbm,
    trim_hbm,
    moduli_hbm,
    band_hbm,
    blocks_hbm,
    basis_hbm,
    inv_hbm,
    out_hbm,
    dpad,
    state,
    mat,
    trim,
    moduli,
    band,
    blk,
    basis,
    inv,
    coef,
    wide,
    own,
    outv,
    row_src,
    row_dst,
    col_src,
    col_dst,
    res_src,
    res_dst,
    sum1_src,
    sum1_dst,
    sum2_src,
    sum2_dst,
    irep,
    load_sem,
    out_sem,
    halo_ssem,
    halo_rsem,
    tan_ssem,
    tan_rsem,
    res_ssem,
    res_rsem,
    sum_ssem,
    sum_rsem,
):
    d = lax.axis_index("prow")
    e = lax.axis_index("pcol")
    up = (lax.rem(d + nrow - 1, nrow), e)
    down = (lax.rem(d + 1, nrow), e)
    left = (d, lax.rem(e + ncol - 1, ncol))
    right = (d, lax.rem(e + 1, ncol))
    rows, cols, ncoarse = 128, 256, 16
    groups = rows // 16

    def load(src, dst, i):
        copy = pltpu.make_async_copy(src, dst, load_sem.at[i])
        copy.start()
        return copy

    l_dir = load(dir_hbm, dpad.at[:, pl.ds(8, rows), :], 0)
    l_state = load(state_hbm, state, 1)
    l_mat = load(mat_hbm, mat, 2)
    l_trim = load(trim_hbm, trim, 3)
    l_mod = load(moduli_hbm, moduli, 4)
    l_basis = load(basis_hbm, basis, 5)
    l_blk = load(blocks_hbm.at[0, 0], blk, 6)
    l_band = load(band_hbm, band, 7)
    l_inv = load(inv_hbm, inv, 8)

    barrier = pltpu.get_barrier_semaphore()
    for k in range(1, ncol):
        pl.semaphore_signal(
            barrier, inc=1, device_id=(d, lax.rem(e + k, ncol)), device_id_type=MESH
        )
    for k in range(1, nrow):
        pl.semaphore_signal(
            barrier, inc=1, device_id=(lax.rem(d + k, nrow), e), device_id_type=MESH
        )

    def send(src, dst, ssem, rsem, to):
        copy = pltpu.make_async_remote_copy(
            src_ref=src, dst_ref=dst, send_sem=ssem, recv_sem=rsem, device_id=to, device_id_type=MESH
        )
        copy.start()
        return copy

    l_dir.wait()
    r16 = iota((16, cols), 0)
    c16 = iota((16, cols), 1)
    edge_cols = jnp.zeros((16, rows), F32)
    for c in range(3):
        pick = ones_where(((r16 == c) & (c16 == 0)) | ((r16 == 8 + c) & (c16 == cols - 1)))
        edge_cols = edge_cols + mm(pick, dpad[c, 8 : 8 + rows, :].astype(BF16), NT)
    col_src[...] = edge_cols
    row_src[...] = jnp.zeros_like(row_src)
    for c in range(3):
        row_src[0, c : c + 1, :] = dpad[c, 8:9, :]
        row_src[1, c : c + 1, :] = dpad[c, 7 + rows : 8 + rows, :]
    pl.semaphore_wait(barrier, ncol - 1 + nrow - 1)
    halo = [
        send(row_src.at[0], row_dst.at[1], halo_ssem.at[0], halo_rsem.at[0], up),
        send(row_src.at[1], row_dst.at[0], halo_ssem.at[1], halo_rsem.at[1], down),
        send(col_src.at[pl.ds(0, 8)], col_dst.at[pl.ds(8, 8)], halo_ssem.at[2], halo_rsem.at[2], left),
        send(col_src.at[pl.ds(8, 8)], col_dst.at[pl.ds(0, 8)], halo_ssem.at[3], halo_rsem.at[3], right),
    ]

    l_state.wait()
    l_mat.wait()
    l_trim.wait()
    l_mod.wait()
    for g in range(groups):
        at = slice(16 * g, 16 * g + 16)
        s0, s1, s2 = state[0, at, :], state[1, at, :], state[2, at, :]
        stretch = 1.0 + 0.3 * (s0 * s0 + s1 * s1 + s2 * s2)
        which = mat[at, :]
        table = jnp.full((16, cols), moduli[0], F32)
        for entry in range(1, 8):
            table = jnp.where(which == entry, moduli[entry], table)
        coef[at, :] = table * (stretch + 1.0 / stretch) * (0.25 + 0.75 * trim[at, :].astype(F32))

    for copy in halo:
        copy.wait_recv()
    row_in = iota((8, cols), 0)
    for c in range(3):
        above = jnp.where(d > 0, row_dst[0, c : c + 1, :], 0.0)
        below = jnp.where(d < nrow - 1, row_dst[1, c : c + 1, :], 0.0)
        dpad[c, 7:8, :] = above
        dpad[c, 8 + rows : 9 + rows, :] = below
    side = iota((16, rows), 0)
    keep = ((side < 8) & (e > 0)) | ((side >= 8) & (e < ncol - 1))
    edges = jnp.where(keep, col_dst[...], 0.0).astype(BF16)
    lane = iota((16, cols), 1)
    tan = []
    for c in range(3):
        place = ones_where(((r16 == c) & (c16 == 0)) | ((r16 == 8 + c) & (c16 == cols - 1)))
        sides = mm(edges, place, TN)
        for g in range(groups):
            r0 = 8 + 16 * g
            centre = dpad[c, r0 : r0 + 16, :]
            beside = dpad[c, r0 - 1 : r0 + 15, :] + dpad[c, r0 + 1 : r0 + 17, :]
            beside = beside + jnp.where(lane == 0, 0.0, pltpu.roll(centre, 1, 1))
            beside = beside + jnp.where(lane == cols - 1, 0.0, pltpu.roll(centre, cols - 1, 1))
            beside = beside + sides[16 * g : 16 * g + 16, :]
            coupled = dpad[(c + 1) % 3, r0 : r0 + 16, :]
            value = coef[16 * g : 16 * g + 16, :] * (5.0 * centre - beside + 0.5 * coupled)
            wide[c, 64 + 16 * g : 80 + 16 * g, :] = value.astype(BF16)
        tan.append(
            (
                send(wide.at[c, pl.ds(64, 64)], wide.at[c, pl.ds(192, 64)], tan_ssem.at[c, 0], tan_rsem.at[c, 0], up),
                send(wide.at[c, pl.ds(128, 64)], wide.at[c, pl.ds(0, 64)], tan_ssem.at[c, 1], tan_rsem.at[c, 1], down),
            )
        )

    l_basis.wait()
    acc = jnp.zeros((48, cols), F32)
    for g in range(groups):
        own_rows = wide[:, 64 + 16 * g : 80 + 16 * g, :].reshape(48, cols)
        functions = basis[:, 16 * g : 16 * g + 16, :].reshape(cols, cols)
        acc = acc + mm(own_rows, functions, NT)
    r48 = iota((48, cols), 0)
    c48 = iota((48, cols), 1)
    same = (r48 % 16) == (c48 % 16)
    acc = jnp.where(same, acc, 0.0)
    high = acc.astype(BF16)
    low = (acc - high.astype(F32)).astype(BF16)
    re = iota((cols, 128), 0)
    ce = iota((cols, 128), 1)
    fold = ones_where(((ce % 16) == (re // 16)) & (ce < 96))
    part = mm(high, fold) + mm(low, fold)
    rp = iota((48, 128), 0)
    cp = iota((48, 128), 1)
    part = jnp.where(((cp // 16) % 3) == (rp // 16), part, 0.0)
    part = jnp.sum(part, axis=0, keepdims=True)
    sum1_src[...] = part
    for k in range(1, ncol):
        send(sum1_src, sum1_dst.at[k - 1], sum_ssem.at[0], sum_rsem.at[0], (d, lax.rem(e + k, ncol)))

    l_blk.wait()
    l_band.wait()
    width = band[0, 0]
    for i in range(8):
        t = iota((32, 256), 0) + 32 * i
        s = iota((32, 256), 1)
        keep = jnp.abs(t - s) <= width
        keep = keep & ((s >= 64) | (d > 0)) & ((s < 192) | (d < nrow - 1))
        keep = keep & ((t >= 64) | (d > 0)) & ((t < 192) | (d < nrow - 1))
        factor = 0.5 if (i < 2 or i >= 6) else 1.0
        factor = jnp.where(keep, factor, 0.0).astype(BF16)
        for c in range(3):
            blk[c, 32 * i : 32 * i + 32, :] = blk[c, 32 * i : 32 * i + 32, :] * factor

    l_inv.wait()
    inv_high = inv[...].astype(BF16)
    inv_low = (inv[...] - inv_high.astype(F32)).astype(BF16)
    repeat = ones_where((iota((48, 768), 1) // 16) == iota((48, 768), 0))
    irep[0:48, :] = mm(inv_high, repeat, TN).astype(BF16)
    irep[48:96, :] = mm(inv_low, repeat, TN).astype(BF16)
    irep[96:128, :] = jnp.zeros((32, 768), BF16)

    def wait_sum(buf, stage):
        pltpu.make_async_remote_copy(
            src_ref=buf, dst_ref=buf, send_sem=sum_ssem.at[stage], recv_sem=sum_rsem.at[stage],
            device_id=right, device_id_type=MESH,
        ).wait()

    wait_sum(sum1_dst, 0)
    part = sum1_src[...] + jnp.sum(sum1_dst[...], axis=0)
    sum2_src[...] = part
    for k in range(1, nrow):
        send(sum2_src, sum2_dst.at[k - 1], sum_ssem.at[1], sum_rsem.at[1], (lax.rem(d + k, nrow), e))

    res = []
    for c in range(3):
        for copy in tan[c]:
            copy.wait()
        vec = wide[c]
        margins = mm(jnp.concatenate([blk[c, 0:64, :], blk[c, 192:256, :]], axis=0), vec)
        res_src[0, c] = margins[0:64, :].astype(BF16)
        res_src[1, c] = margins[64:128, :].astype(BF16)
        res.append(
            (
                send(res_src.at[0, c], res_dst.at[1, c], res_ssem.at[c, 0], res_rsem.at[c, 0], up),
                send(res_src.at[1, c], res_dst.at[0, c], res_ssem.at[c, 1], res_rsem.at[c, 1], down),
            )
        )
        own[c] = mm(blk[c, 64:192, :], vec)

    wait_sum(sum2_dst, 1)
    total = sum2_src[...] + jnp.sum(sum2_dst[...], axis=0)
    total = jnp.broadcast_to(total, (16, 128))
    high = total.astype(BF16).astype(F32)
    mid = (total - high).astype(BF16).astype(F32)
    low = total - high - mid
    rt = iota((16, 128), 0)
    split = jnp.where(rt == 0, high, jnp.where(rt == 1, mid, jnp.where(rt == 2, low, 0.0))).astype(BF16)
    step = jnp.sum(mm(split, irep[...]), axis=0, keepdims=True)
    step = step.astype(BF16).astype(F32)
    spread = jnp.concatenate(
        [jnp.broadcast_to(step[:, c * cols : c * cols + cols], (16, cols)) for c in range(3)], axis=0
    )
    spread = jnp.where(same, spread, 0.0).astype(BF16)
    for g in range(groups):
        functions = basis[:, 16 * g : 16 * g + 16, :].reshape(cols, cols)
        term = mm(spread, functions)
        for c in range(3):
            at = slice(16 * g, 16 * g + 16)
            own[c, at, :] = own[c, at, :] + term[16 * c : 16 * c + 16, :]

    writes = []
    for c in range(3):
        for copy in res[c]:
            copy.wait()
        outv[c, 0:64, :] = own[c, 0:64, :] + res_dst[0, c].astype(F32)
        outv[c, 64:128, :] = own[c, 64:128, :] + res_dst[1, c].astype(F32)
        copy = pltpu.make_async_copy(outv.at[c], out_hbm.at[c], out_sem.at[c])
        copy.start()
        writes.append(copy)
    for copy in halo:
        copy.wait_send()
    for copy in writes:
        copy.wait()


def body(nrow, ncol, *args):
    vm = pltpu.VMEM
    dma = pltpu.SemaphoreType.DMA
    return pl.pallas_call(
        functools.partial(kernel, nrow, ncol),
        out_shape=jax.ShapeDtypeStruct((3, 128, 256), F32),
        in_specs=[pl.BlockSpec(memory_space=pl.ANY)] * 9,
        out_specs=pl.BlockSpec(memory_space=pl.ANY),
        scratch_shapes=[
            vm((3, 144, 256), F32),
            vm((3, 128, 256), F32),
            vm((128, 256), jnp.int32),
            vm((128, 256), jnp.int32),
            pltpu.SMEM((8,), F32),
            pltpu.SMEM((1, 1), jnp.int32),
            vm((3, 256, 256), BF16),
            vm((16, 128, 256), BF16),
            vm((48, 48), F32),
            vm((128, 256), F32),
            vm((3, 256, 256), BF16),
            vm((3, 128, 256), F32),
            vm((3, 128, 256), F32),
            vm((2, 8, 256), F32),
            vm((2, 8, 256), F32),
            vm((16, 128), F32),
            vm((16, 128), F32),
            vm((2, 3, 64, 256), BF16),
            vm((2, 3, 64, 256), BF16),
            vm((1, 128), F32),
            vm((ncol - 1, 1, 128), F32),
            vm((1, 128), F32),
            vm((nrow - 1, 1, 128), F32),
            vm((128, 768), BF16),
            dma((9,)),
            dma((3,)),
            dma((4,)),
            dma((4,)),
            dma((3, 2)),
            dma((3, 2)),
            dma((3, 2)),
            dma((3, 2)),
            dma((2,)),
            dma((2,)),
        ],
        compiler_params=pltpu.CompilerParams(
            collective_id=0, has_side_effects=True, vmem_limit_bytes=40 * 1024 * 1024
        ),
        name="schwarz",
    )(*args)


def solution(mesh):
    placed = (
        P(None, "prow", "pcol"),
        P(None, "prow", "pcol"),
        P("prow", "pcol"),
        P("prow", "pcol"),
        P(),
        P("prow", "pcol"),
        P("prow", "pcol", None, None, None),
        P(None, "prow", "pcol"),
        P(),
    )
    return jax.shard_map(
        functools.partial(body, mesh.shape["prow"], mesh.shape["pcol"]),
        mesh=mesh,
        in_specs=placed,
        out_specs=P(None, "prow", "pcol"),
        check_vma=False,
    )
```

```python
import functools

import jax
import jax.numpy as jnp
from jax import lax
from jax.experimental import pallas as pl
from jax.experimental.pallas import tpu as pltpu
from jax.sharding import PartitionSpec as P

MESH = pl.DeviceIdType.MESH
F32 = jnp.float32
BF16 = jnp.bfloat16
NT = (((1,), (1,)), ((), ()))
TN = (((0,), (0,)), ((), ()))


def iota(shape, dim):
    return lax.broadcasted_iota(jnp.int32, shape, dim)


def mm(a, b, dims=(((1,), (0,)), ((), ()))):
    return lax.dot_general(a, b, dims, preferred_element_type=F32)


def ones_where(cond):
    return jnp.where(cond, 1.0, 0.0).astype(BF16)


def far_first(n, dist):
    return sorted(range(1, n), key=lambda k: (-dist(k), k))


def ring(k, n):
    return min(k % n, n - k % n)


def prow_distance(k, n):
    hops = 0
    for x in range(4):
        hops += ring((x + k) % 4 - x, 4) + ring((x + k) // 4, max(n // 4, 1))
    return hops


def kernel(
    nrow,
    ncol,
    dir_hbm,
    state_hbm,
    mat_hbm,
    trim_hbm,
    moduli_hbm,
    band_hbm,
    blocks_hbm,
    basis_hbm,
    inv_hbm,
    out,
    dpad,
    state,
    mat,
    trim,
    moduli,
    band,
    blk,
    basis,
    inv,
    coef,
    wide,
    own,
    row_dst,
    col_src,
    col_dst,
    res_src,
    res_dst,
    sum1_src,
    sum1_dst,
    sum2_src,
    sum2_dst,
    irep,
    load_sem,
    halo_ssem,
    halo_rsem,
    tan_ssem,
    tan_rsem,
    res_ssem,
    res_rsem,
    sum_ssem,
    sum_rsem,
    entry_sem,
):
    d = lax.axis_index("prow")
    e = lax.axis_index("pcol")

    def row_at(k):
        return (lax.rem(d + (k + nrow) % nrow, nrow), e)

    def col_at(k):
        return (d, lax.rem(e + (k + ncol) % ncol, ncol))

    up, down, left, right = row_at(-1), row_at(1), col_at(-1), col_at(1)
    rows, cols = 128, 256
    groups = rows // 16

    def signal(sem, to):
        pl.semaphore_signal(sem, inc=1, device_id=to, device_id_type=MESH)

    barrier = pltpu.get_barrier_semaphore()
    for to in (up, down, left, right):
        signal(barrier, to)

    def load(src, dst, i):
        copy = pltpu.make_async_copy(src, dst, load_sem.at[i])
        copy.start()
        return copy

    l_dir = load(dir_hbm, dpad.at[:, pl.ds(8, rows), :], 0)
    l_state = load(state_hbm, state, 1)
    l_mat = load(mat_hbm, mat, 2)
    l_trim = load(trim_hbm, trim, 3)
    l_mod = load(moduli_hbm, moduli, 4)
    l_blk = load(blocks_hbm.at[0, 0], blk, 6)
    l_band = load(band_hbm, band, 7)
    l_inv = load(inv_hbm, inv, 8)
    l_basis = load(basis_hbm, basis, 5)

    def send(src, dst, ssem, rsem, to):
        copy = pltpu.make_async_remote_copy(
            src_ref=src, dst_ref=dst, send_sem=ssem, recv_sem=rsem, device_id=to, device_id_type=MESH
        )
        copy.start()
        return copy

    def tell(level):
        step = 1 << level
        sem = entry_sem.at[level]
        count = 0
        if step < nrow // 2:
            signal(sem, row_at(step))
            signal(sem, row_at(-step))
            count += 2
        if step < ncol // 2:
            signal(sem, col_at(step))
            signal(sem, col_at(-step))
            count += 2
        return count

    def hear(level, count):
        if count:
            pl.semaphore_wait(entry_sem.at[level], count)

    l_dir.wait()
    pl.semaphore_wait(barrier, 4)
    halo = [
        send(dpad.at[:, pl.ds(8, 8)], row_dst.at[1], halo_ssem.at[0], halo_rsem.at[0], up),
        send(dpad.at[:, pl.ds(rows, 8)], row_dst.at[0], halo_ssem.at[1], halo_rsem.at[1], down),
    ]
    told = tell(0)
    r16 = iota((16, cols), 0)
    c16 = iota((16, cols), 1)
    edge_cols = jnp.zeros((16, rows), F32)
    for c in range(3):
        pick = ones_where(((r16 == c) & (c16 == 0)) | ((r16 == 8 + c) & (c16 == cols - 1)))
        edge_cols = edge_cols + mm(pick, dpad[c, 8 : 8 + rows, :].astype(BF16), NT)
    col_src[...] = edge_cols
    halo += [
        send(col_src.at[pl.ds(0, 8)], col_dst.at[pl.ds(8, 8)], halo_ssem.at[2], halo_rsem.at[2], left),
        send(col_src.at[pl.ds(8, 8)], col_dst.at[pl.ds(0, 8)], halo_ssem.at[3], halo_rsem.at[3], right),
    ]

    l_state.wait()
    l_mat.wait()
    l_trim.wait()
    l_mod.wait()
    for g in range(groups):
        at = slice(16 * g, 16 * g + 16)
        s0, s1, s2 = state[0, at, :], state[1, at, :], state[2, at, :]
        stretch = 1.0 + 0.3 * (s0 * s0 + s1 * s1 + s2 * s2)
        which = mat[at, :]
        table = jnp.full((16, cols), moduli[0], F32)
        for entry in range(1, 8):
            table = jnp.where(which == entry, moduli[entry], table)
        coef[at, :] = table * (stretch + 1.0 / stretch) * (0.25 + 0.75 * trim[at, :].astype(F32))

    hear(0, told)
    told = tell(1)

    l_blk.wait()
    l_band.wait()
    width = band[0, 0]
    for i in range(8):
        t = iota((32, 256), 0) + 32 * i
        s = iota((32, 256), 1)
        keep = jnp.abs(t - s) <= width
        keep = keep & ((s >= 64) | (d > 0)) & ((s < 192) | (d < nrow - 1))
        keep = keep & ((t >= 64) | (d > 0)) & ((t < 192) | (d < nrow - 1))
        factor = 0.5 if (i < 2 or i >= 6) else 1.0
        factor = jnp.where(keep, factor, 0.0).astype(BF16)
        for c in range(3):
            blk[c, 32 * i : 32 * i + 32, :] = blk[c, 32 * i : 32 * i + 32, :] * factor

    l_inv.wait()
    inv_high = inv[...].astype(BF16)
    inv_low = (inv[...] - inv_high.astype(F32)).astype(BF16)
    repeat = ones_where((iota((48, 768), 1) // 16) == iota((48, 768), 0))
    irep[0:48, :] = mm(inv_high, repeat, TN).astype(BF16)
    irep[48:96, :] = mm(inv_low, repeat, TN).astype(BF16)
    irep[96:128, :] = jnp.zeros((32, 768), BF16)

    hear(1, told)
    told = tell(2)

    l_basis.wait()
    for copy in halo:
        copy.wait_recv()
    for c in range(3):
        dpad[c, 7:8, :] = jnp.where(d > 0, row_dst[0, c, 7:8, :], 0.0)
        dpad[c, 8 + rows : 9 + rows, :] = jnp.where(d < nrow - 1, row_dst[1, c, 0:1, :], 0.0)
    side = iota((16, rows), 0)
    keep = ((side < 8) & (e > 0)) | ((side >= 8) & (e < ncol - 1))
    edges = jnp.where(keep, col_dst[...], 0.0).astype(BF16)
    lane = iota((16, cols), 1)
    tan = []
    for c in range(3):
        place = ones_where(((r16 == c) & (c16 == 0)) | ((r16 == 8 + c) & (c16 == cols - 1)))
        sides = mm(edges, place, TN)
        for g in range(groups):
            r0 = 8 + 16 * g
            centre = dpad[c, r0 : r0 + 16, :]
            beside = dpad[c, r0 - 1 : r0 + 15, :] + dpad[c, r0 + 1 : r0 + 17, :]
            beside = beside + jnp.where(lane == 0, 0.0, pltpu.roll(centre, 1, 1))
            beside = beside + jnp.where(lane == cols - 1, 0.0, pltpu.roll(centre, cols - 1, 1))
            beside = beside + sides[16 * g : 16 * g + 16, :]
            coupled = dpad[(c + 1) % 3, r0 : r0 + 16, :]
            value = coef[16 * g : 16 * g + 16, :] * (5.0 * centre - beside + 0.5 * coupled)
            wide[c, 64 + 16 * g : 80 + 16 * g, :] = value.astype(BF16)
        tan.append(
            (
                send(wide.at[c, pl.ds(64, 64)], wide.at[c, pl.ds(192, 64)], tan_ssem.at[c, 0], tan_rsem.at[c, 0], up),
                send(wide.at[c, pl.ds(128, 64)], wide.at[c, pl.ds(0, 64)], tan_ssem.at[c, 1], tan_rsem.at[c, 1], down),
            )
        )

    acc = jnp.zeros((48, cols), F32)
    for g in range(groups):
        own_rows = wide[:, 64 + 16 * g : 80 + 16 * g, :].reshape(48, cols)
        functions = basis[:, 16 * g : 16 * g + 16, :].reshape(cols, cols)
        acc = acc + mm(own_rows, functions, NT)
    r48 = iota((48, cols), 0)
    c48 = iota((48, cols), 1)
    same = (r48 % 16) == (c48 % 16)
    acc = jnp.where(same, acc, 0.0)
    high = acc.astype(BF16)
    low = (acc - high.astype(F32)).astype(BF16)
    re = iota((cols, 128), 0)
    ce = iota((cols, 128), 1)
    fold = ones_where(((ce % 16) == (re // 16)) & (ce < 96))
    part = mm(high, fold) + mm(low, fold)
    rp = iota((48, 128), 0)
    cp = iota((48, 128), 1)
    part = jnp.where(((cp // 16) % 3) == (rp // 16), part, 0.0)
    sum1_src[...] = jnp.sum(part, axis=0, keepdims=True)
    hear(2, told)
    told = tell(3)
    for k in far_first(ncol, lambda k: ring(k, ncol)):
        send(sum1_src, sum1_dst.at[k - 1], sum_ssem.at[0], sum_rsem.at[0], col_at(k))

    def whole(buf, stage):
        return pltpu.make_async_remote_copy(
            src_ref=buf, dst_ref=buf, send_sem=sum_ssem.at[stage], recv_sem=sum_rsem.at[stage],
            device_id=right, device_id_type=MESH,
        )

    res = []

    def local(c):
        for copy in tan[c]:
            copy.wait_recv()
        vec = wide[c]
        margins = mm(jnp.concatenate([blk[c, 0:64, :], blk[c, 192:256, :]], axis=0), vec)
        res_src[0, c] = margins[0:64, :].astype(BF16)
        res_src[1, c] = margins[64:128, :].astype(BF16)
        res.append(
            (
                send(res_src.at[0, c], res_dst.at[1, c], res_ssem.at[c, 0], res_rsem.at[c, 0], up),
                send(res_src.at[1, c], res_dst.at[0, c], res_ssem.at[c, 1], res_rsem.at[c, 1], down),
            )
        )
        own[c] = mm(blk[c, 64:192, :], vec)

    local(0)

    whole(sum1_dst, 0).wait_recv()
    sum2_src[...] = sum1_src[...] + jnp.sum(sum1_dst[...], axis=0)
    hear(3, told)
    for k in far_first(nrow, lambda k: prow_distance(k, nrow)):
        send(sum2_src, sum2_dst.at[k - 1], sum_ssem.at[1], sum_rsem.at[1], row_at(k))

    local(1)
    local(2)

    for c in range(3):
        for copy in res[c]:
            copy.wait_recv()
        own[c, 0:64, :] = own[c, 0:64, :] + res_dst[0, c].astype(F32)
        own[c, 64:128, :] = own[c, 64:128, :] + res_dst[1, c].astype(F32)

    whole(sum2_dst, 1).wait_recv()
    total = sum2_src[...] + jnp.sum(sum2_dst[...], axis=0)
    total = jnp.broadcast_to(total, (16, 128))
    high = total.astype(BF16).astype(F32)
    mid = (total - high).astype(BF16).astype(F32)
    low = total - high - mid
    rt = iota((16, 128), 0)
    split = jnp.where(rt == 0, high, jnp.where(rt == 1, mid, jnp.where(rt == 2, low, 0.0))).astype(BF16)
    step = jnp.sum(mm(split, irep[...]), axis=0, keepdims=True)
    step = step.astype(BF16).astype(F32)
    spread = jnp.concatenate(
        [jnp.broadcast_to(step[:, c * cols : c * cols + cols], (16, cols)) for c in range(3)], axis=0
    )
    spread = jnp.where(same, spread, 0.0).astype(BF16)
    for g in range(groups):
        at = slice(16 * g, 16 * g + 16)
        term = mm(spread, basis[:, at, :].reshape(cols, cols))
        for c in range(3):
            out[c, at, :] = own[c, at, :] + term[16 * c : 16 * c + 16, :]
    for copy in halo:
        copy.wait_send()
    for c in range(3):
        for copy in tan[c] + res[c]:
            copy.wait_send()
    whole(sum1_dst, 0).wait_send()
    whole(sum2_dst, 1).wait_send()


def body(nrow, ncol, *args):
    vm = pltpu.VMEM
    dma = pltpu.SemaphoreType.DMA
    return pl.pallas_call(
        functools.partial(kernel, nrow, ncol),
        out_shape=vm((3, 128, 256), F32),
        in_specs=[pl.BlockSpec(memory_space=pltpu.HBM)] * 9,
        out_specs=pl.BlockSpec(memory_space=vm),
        scratch_shapes=[
            vm((3, 144, 256), F32),
            vm((3, 128, 256), F32),
            vm((128, 256), jnp.int32),
            vm((128, 256), jnp.int32),
            pltpu.SMEM((8,), F32),
            pltpu.SMEM((1, 1), jnp.int32),
            vm((3, 256, 256), BF16),
            vm((16, 128, 256), BF16),
            vm((48, 48), F32),
            vm((128, 256), F32),
            vm((3, 256, 256), BF16),
            vm((3, 128, 256), F32),
            vm((2, 3, 8, 256), F32),
            vm((16, 128), F32),
            vm((16, 128), F32),
            vm((2, 3, 64, 256), BF16),
            vm((2, 3, 64, 256), BF16),
            vm((1, 128), F32),
            vm((ncol - 1, 1, 128), F32),
            vm((1, 128), F32),
            vm((nrow - 1, 1, 128), F32),
            vm((128, 768), BF16),
            dma((9,)),
            dma((4,)),
            dma((4,)),
            dma((3, 2)),
            dma((3, 2)),
            dma((3, 2)),
            dma((3, 2)),
            dma((2,)),
            dma((2,)),
            pltpu.SemaphoreType.REGULAR((4,)),
        ],
        compiler_params=pltpu.CompilerParams(
            collective_id=0, has_side_effects=True, vmem_limit_bytes=56 * 1024 * 1024
        ),
        name="schwarz",
    )(*args)


def solution(mesh):
    placed = (
        P(None, "prow", "pcol"),
        P(None, "prow", "pcol"),
        P("prow", "pcol"),
        P("prow", "pcol"),
        P(),
        P("prow", "pcol"),
        P("prow", "pcol", None, None, None),
        P(None, "prow", "pcol"),
        P(),
    )
    return jax.shard_map(
        functools.partial(body, mesh.shape["prow"], mesh.shape["pcol"]),
        mesh=mesh,
        in_specs=placed,
        out_specs=P(None, "prow", "pcol"),
        check_vma=False,
    )
```

```python
import functools

import jax
import jax.numpy as jnp
from jax import lax
from jax.experimental import pallas as pl
from jax.experimental.pallas import tpu as pltpu
from jax.sharding import PartitionSpec as P

MESH = pl.DeviceIdType.MESH
F32 = jnp.float32
BF16 = jnp.bfloat16
NT = (((1,), (1,)), ((), ()))
TN = (((0,), (0,)), ((), ()))


def iota(shape, dim):
    return lax.broadcasted_iota(jnp.int32, shape, dim)


def mm(a, b, dims=(((1,), (0,)), ((), ()))):
    return lax.dot_general(a, b, dims, preferred_element_type=F32)


def ones_where(cond):
    return jnp.where(cond, 1.0, 0.0).astype(BF16)


def ring(k, n):
    return min(k % n, n - k % n)


def near_set(xs, ys, reach):
    found = [(dx, dy) for dx in range(xs) for dy in range(ys) if 0 < ring(dx, xs) + ring(dy, ys) <= reach]
    return sorted(found, key=lambda o: (ring(o[0], xs) + ring(o[1], ys), o))


def sums_of(first, second, xs, ys):
    second = set(second) | {(0, 0)}
    return {((a + c) % xs, (b + f) % ys) for a, b in first for c, f in second}


def entry_plan(xs, ys):
    origin = {(0, 0)}
    greet = {(dx % xs, dy % ys) for dx, dy in ((1, 0), (-1, 0), (0, 1), (0, -1), (1, 1), (-1, -1))} - origin
    known = greet | origin
    levels = []
    while len(known) < xs * ys:
        if not levels:
            told = {(1 % xs, 0), (-1 % xs, 0), (0, 1 % ys), (0, -1 % ys)}
        elif len(levels) == 1:
            told = {(xs // 2, 0), (0, 2 % ys), (0, -2 % ys)}
        else:
            told = {(0, 2 % ys), (0, -2 % ys)}
        told = sorted(told - origin)
        levels.append(told)
        known = sums_of(known, told, xs, ys)
    return sorted(greet), levels


def line_plan(n):
    greet = [k for k in sorted(range(1, n), key=lambda k: (ring(k, n), k)) if ring(k, n) <= 2]
    levels, reach = [], 2
    while reach < n // 2:
        levels.append([reach, n - reach])
        reach *= 2
    return greet, levels


def kernel(
    nrow,
    ncol,
    dir_hbm,
    state_hbm,
    mat_hbm,
    trim_hbm,
    moduli_hbm,
    band_hbm,
    blocks_hbm,
    basis_hbm,
    inv_hbm,
    out,
    dpad,
    state,
    mat,
    trim,
    moduli,
    band,
    blk,
    basis,
    inv,
    coef,
    wide,
    own,
    row_src,
    row_dst,
    col_src,
    col_dst,
    res_src,
    res_dst,
    sum1_src,
    sum1_dst,
    sum2_src,
    sum2_dst,
    irep,
    place,
    inner,
    fix_src,
    fix_dst,
    edge_rows,
    edge_functions,
    load_sem,
    halo_ssem,
    halo_rsem,
    tan_ssem,
    tan_rsem,
    fix_ssem,
    fix_rsem,
    res_ssem,
    res_rsem,
    sum_ssem,
    sum_rsem,
    entry_sem,
):
    d = lax.axis_index("prow")
    e = lax.axis_index("pcol")

    def col_at(k):
        return (d, lax.rem(e + k % ncol, ncol))

    xs, ys = 4, nrow // 4
    x = lax.rem(d, xs)
    y = d // xs

    def row_at(offset):
        dx, dy = offset
        return (lax.rem(y + dy, ys) * xs + lax.rem(x + dx, xs), e)

    up, down = (lax.rem(d + nrow - 1, nrow), e), (lax.rem(d + 1, nrow), e)
    left, right = col_at(-1), col_at(1)
    rows, cols = 128, 256
    groups = rows // 16

    def signal(sem, to):
        pl.semaphore_signal(sem, inc=1, device_id=to, device_id_type=MESH)

    row_greet, row_levels = entry_plan(xs, ys)
    col_greet, col_levels = line_plan(ncol)
    barrier = pltpu.get_barrier_semaphore()
    for offset in row_greet:
        signal(barrier, row_at(offset))
    for k in col_greet:
        signal(barrier, col_at(k))

    def load(src, dst, i):
        copy = pltpu.make_async_copy(src, dst, load_sem.at[i])
        copy.start()
        return copy

    l_dir = load(dir_hbm, dpad.at[:, pl.ds(8, rows), :], 0)
    l_state = load(state_hbm, state, 1)
    l_mat = load(mat_hbm, mat, 2)
    l_trim = load(trim_hbm, trim, 3)
    l_mod = load(moduli_hbm, moduli, 4)
    l_blk = load(blocks_hbm.at[0, 0], blk, 6)
    l_band = load(band_hbm, band, 7)
    l_inv = load(inv_hbm, inv, 8)
    l_basis = load(basis_hbm, basis, 5)

    def send(src, dst, ssem, rsem, to):
        copy = pltpu.make_async_remote_copy(
            src_ref=src, dst_ref=dst, send_sem=ssem, recv_sem=rsem, device_id=to, device_id_type=MESH
        )
        copy.start()
        return copy

    def tell(level):
        count = 0
        for levels, at in ((row_levels, row_at), (col_levels, col_at)):
            if level < len(levels):
                for k in levels[level]:
                    signal(entry_sem.at[level], at(k))
                count += len(levels[level])
        return count

    def hear(level, count):
        if count:
            pl.semaphore_wait(entry_sem.at[level], count)

    r16 = iota((16, cols), 0)
    c16 = iota((16, cols), 1)
    l_dir.wait()
    row_src[...] = jnp.zeros_like(row_src)
    edge_cols = jnp.zeros((16, rows), F32)
    for c in range(3):
        row_src[0, c : c + 1, :] = dpad[c, 8:9, :]
        row_src[1, c : c + 1, :] = dpad[c, 7 + rows : 8 + rows, :]
        pick = ones_where(((r16 == c) & (c16 == 0)) | ((r16 == 8 + c) & (c16 == cols - 1)))
        place[c] = pick
        edge_cols = edge_cols + mm(pick, dpad[c, 8 : 8 + rows, :].astype(BF16), NT)
    col_src[...] = edge_cols
    pl.semaphore_wait(barrier, len(row_greet) + len(col_greet))
    halo = [
        send(row_src.at[0], row_dst.at[1], halo_ssem.at[0], halo_rsem.at[0], up),
        send(row_src.at[1], row_dst.at[0], halo_ssem.at[1], halo_rsem.at[1], down),
        send(col_src.at[pl.ds(0, 8)], col_dst.at[pl.ds(8, 8)], halo_ssem.at[2], halo_rsem.at[2], left),
        send(col_src.at[pl.ds(8, 8)], col_dst.at[pl.ds(0, 8)], halo_ssem.at[3], halo_rsem.at[3], right),
    ]
    told = tell(0)

    l_state.wait()
    l_mat.wait()
    l_trim.wait()
    l_mod.wait()
    for g in range(groups):
        at = slice(16 * g, 16 * g + 16)
        s0, s1, s2 = state[0, at, :], state[1, at, :], state[2, at, :]
        stretch = 1.0 + 0.3 * (s0 * s0 + s1 * s1 + s2 * s2)
        which = mat[at, :]
        table = jnp.full((16, cols), moduli[0], F32)
        for entry in range(1, 8):
            table = jnp.where(which == entry, moduli[entry], table)
        coef[at, :] = table * (stretch + 1.0 / stretch) * (0.25 + 0.75 * trim[at, :].astype(F32))

    lane = iota((16, cols), 1)
    side = iota((16, cols), 0)
    zero_row = jnp.zeros((1, cols), F32)
    tan = []
    for c in range(3):
        dpad[c, 7:8, :] = zero_row
        dpad[c, 8 + rows : 9 + rows, :] = zero_row
        for g in range(groups):
            r0 = 8 + 16 * g
            at = slice(16 * g, 16 * g + 16)
            centre = dpad[c, r0 : r0 + 16, :]
            beside = dpad[c, r0 - 1 : r0 + 15, :] + dpad[c, r0 + 1 : r0 + 17, :]
            beside = beside + jnp.where(lane == 0, 0.0, pltpu.roll(centre, 1, 1))
            beside = beside + jnp.where(lane == cols - 1, 0.0, pltpu.roll(centre, cols - 1, 1))
            coupled = dpad[(c + 1) % 3, r0 : r0 + 16, :]
            value = coef[at, :] * (5.0 * centre - beside + 0.5 * coupled)
            own[c, at, :] = value
            inner[c, at, :] = value.astype(BF16)
        tan.append(
            (
                send(inner.at[c, pl.ds(0, 64)], wide.at[c, pl.ds(192, 64)], tan_ssem.at[c, 0], tan_rsem.at[c, 0], up),
                send(inner.at[c, pl.ds(64, 64)], wide.at[c, pl.ds(0, 64)], tan_ssem.at[c, 1], tan_rsem.at[c, 1], down),
            )
        )

    coef_high = coef[...].astype(BF16)
    coef_low = (coef[...] - coef_high.astype(F32)).astype(BF16)
    both = ones_where(((r16 < 8) & (c16 == 0)) | ((r16 >= 8) & (c16 == cols - 1)))
    coef_cols = mm(both, coef_high, NT) + mm(both, coef_low, NT)

    hear(0, told)
    told = tell(1)

    halo[2].wait_recv()
    halo[3].wait_recv()
    half = iota((16, rows), 0)
    keep = ((half < 8) & (e > 0)) | ((half >= 8) & (e < ncol - 1))
    shares = -coef_cols * jnp.where(keep, col_dst[...], 0.0)
    for i in range(2):
        fix_src[i, 0:16, :] = shares
        edge = coef[(rows - 1) * i : (rows - 1) * i + 1, :]
        fix_src[i, 16:24, :] = jnp.concatenate(
            [jnp.broadcast_to(edge[:, 0:128], (4, 128)), jnp.broadcast_to(edge[:, 128:256], (4, 128))], axis=0
        )
    fix = [
        send(fix_src.at[0], fix_dst.at[1], fix_ssem.at[0], fix_rsem.at[0], up),
        send(fix_src.at[1], fix_dst.at[0], fix_ssem.at[1], fix_rsem.at[1], down),
    ]

    l_basis.wait()
    r48 = iota((48, cols), 0)
    c48 = iota((48, cols), 1)
    same = (r48 % 16) == (c48 % 16)
    re = iota((cols, 128), 0)
    ce = iota((cols, 128), 1)
    fold = ones_where(((ce % 16) == (re // 16)) & (ce < 96))
    rp = iota((48, 128), 0)
    cp = iota((48, 128), 1)
    rh = iota((16, 128), 0)
    ch = iota((16, 128), 1)
    mine = (((ch // 16) % 3) == (rh % 8)) & (rh % 8 < 3) & (ch < 96)

    for c in range(3):
        sides = mm(shares.astype(BF16), place[c], TN)
        for g in range(groups):
            at = slice(16 * g, 16 * g + 16)
            value = own[c, at, :] + sides[at, :]
            own[c, at, :] = value
            wide[c, 64 + 16 * g : 80 + 16 * g, :] = value.astype(BF16)
    acc = jnp.zeros((48, cols), F32)
    for g in range(groups):
        own_rows = wide[:, 64 + 16 * g : 80 + 16 * g, :].reshape(48, cols)
        functions = basis[:, 16 * g : 16 * g + 16, :].reshape(cols, cols)
        acc = acc + mm(own_rows, functions, NT)
    acc = jnp.where(same, acc, 0.0)
    high = acc.astype(BF16)
    low = (acc - high.astype(F32)).astype(BF16)
    part = mm(high, fold) + mm(low, fold)
    part = jnp.where((((cp // 16) % 3) == (rp // 16)) & (cp < 96), part, 0.0)
    sum1_src[...] = jnp.sum(part, axis=0, keepdims=True)
    for k in range(16):
        for i in range(2):
            edge_rows[i, k : k + 1, :] = basis[k, (rows - 16) * i : (rows - 16) * i + 16, :].astype(F32)[15 * i : 15 * i + 1, :]
    for i in range(2):
        one = edge_rows[i].astype(BF16)
        for j in range(6):
            edge_functions[i, 16 * j : 16 * j + 16, :] = one
        edge_functions[i, 96:128, :] = jnp.zeros((32, cols), BF16)

    l_blk.wait()
    l_band.wait()
    width = band[0, 0]
    for i in range(8):
        t = iota((32, 256), 0) + 32 * i
        s = iota((32, 256), 1)
        keep = jnp.abs(t - s) <= width
        keep = keep & ((s >= 64) | (d > 0)) & ((s < 192) | (d < nrow - 1))
        keep = keep & ((t >= 64) | (d > 0)) & ((t < 192) | (d < nrow - 1))
        factor = 0.5 if (i < 2 or i >= 6) else 1.0
        factor = jnp.where(keep, factor, 0.0).astype(BF16)
        for c in range(3):
            blk[c, 32 * i : 32 * i + 32, :] = blk[c, 32 * i : 32 * i + 32, :] * factor

    l_inv.wait()
    inv_high = inv[...].astype(BF16)
    inv_low = (inv[...] - inv_high.astype(F32)).astype(BF16)
    repeat = ones_where((iota((48, 768), 1) // 16) == iota((48, 768), 0))
    irep[0:48, :] = mm(inv_high, repeat, TN).astype(BF16)
    irep[48:96, :] = mm(inv_low, repeat, TN).astype(BF16)
    irep[96:128, :] = jnp.zeros((32, 768), BF16)

    hear(1, told)
    told = tell(2)

    halo[0].wait_recv()
    halo[1].wait_recv()
    above = jnp.where(d > 0, row_dst[0], 0.0) * -coef[0:1, :]
    below = jnp.where(d < nrow - 1, row_dst[1], 0.0) * -coef[rows - 1 : rows, :]
    rim = jnp.concatenate([above, below], axis=0).astype(BF16)
    part = jnp.where(rh < 8, mm(rim, edge_functions[0], NT), mm(rim, edge_functions[1], NT))
    part = jnp.where(mine, part, 0.0)
    sum1_src[...] = sum1_src[...] + jnp.sum(part, axis=0, keepdims=True)
    for k in sorted(range(1, ncol), key=lambda k: (-ring(k, ncol), k)):
        send(sum1_src, sum1_dst.at[k - 1], sum_ssem.at[0], sum_rsem.at[0], col_at(k))

    for c in range(3):
        first = own[c, 0:16, :] + jnp.where(side == 0, above[c : c + 1, :], 0.0)
        last = own[c, rows - 16 : rows, :] + jnp.where(side == 15, below[c : c + 1, :], 0.0)
        wide[c, 64:80, :] = first.astype(BF16)
        wide[c, 48 + rows : 64 + rows, :] = last.astype(BF16)

    def whole(buf, stage):
        return pltpu.make_async_remote_copy(
            src_ref=buf, dst_ref=buf, send_sem=sum_ssem.at[stage], recv_sem=sum_rsem.at[stage],
            device_id=right, device_id_type=MESH,
        )

    res = []

    def local(c):
        for copy in tan[c]:
            copy.wait_recv()
        if c == 0:
            for copy in fix:
                copy.wait_recv()
        for i in range(2):
            sides = mm(fix_dst[i, 0:16, :].astype(BF16), place[c], TN)
            edge = jnp.concatenate([fix_dst[i, 16:17, :], fix_dst[i, 20:21, :]], axis=1)
            beyond = dpad[c, 8:9, :] if i == 0 else dpad[c, 7 + rows : 8 + rows, :]
            for j in range(4):
                to = slice(192 * i + 16 * j, 192 * i + 16 * j + 16)
                lines = slice(64 * (1 - i) + 16 * j, 64 * (1 - i) + 16 * j + 16)
                value = wide[c, to, :].astype(F32) + sides[lines, :]
                if j == (3 if i == 0 else 0):
                    value = value - jnp.where(side == (15 if i == 0 else 0), edge * beyond, 0.0)
                wide[c, to, :] = value.astype(BF16)
        vec = wide[c]
        margins = mm(jnp.concatenate([blk[c, 0:64, :], blk[c, 192:256, :]], axis=0), vec)
        res_src[0, c] = margins[0:64, :].astype(BF16)
        res_src[1, c] = margins[64:128, :].astype(BF16)
        res.append(
            (
                send(res_src.at[0, c], res_dst.at[1, c], res_ssem.at[c, 0], res_rsem.at[c, 0], up),
                send(res_src.at[1, c], res_dst.at[0, c], res_ssem.at[c, 1], res_rsem.at[c, 1], down),
            )
        )
        own[c] = mm(blk[c, 64:192, :], vec)

    local(0)

    whole(sum1_dst, 0).wait_recv()
    sum2_src[...] = sum1_src[...] + jnp.sum(sum1_dst[...], axis=0)
    hear(2, told)
    for offset in reversed(near_set(xs, ys, nrow)):
        slot = offset[1] * xs + offset[0] - 1
        send(sum2_src, sum2_dst.at[slot], sum_ssem.at[1], sum_rsem.at[1], row_at(offset))

    local(1)
    local(2)

    for c in range(3):
        for copy in res[c]:
            copy.wait_recv()
        own[c, 0:64, :] = own[c, 0:64, :] + res_dst[0, c].astype(F32)
        own[c, 64:128, :] = own[c, 64:128, :] + res_dst[1, c].astype(F32)

    whole(sum2_dst, 1).wait_recv()
    total = sum2_src[...] + jnp.sum(sum2_dst[...], axis=0)
    total = jnp.broadcast_to(total, (16, 128))
    high = total.astype(BF16).astype(F32)
    mid = (total - high).astype(BF16).astype(F32)
    low = total - high - mid
    rt = iota((16, 128), 0)
    split = jnp.where(rt == 0, high, jnp.where(rt == 1, mid, jnp.where(rt == 2, low, 0.0))).astype(BF16)
    step = jnp.sum(mm(split, irep[...]), axis=0, keepdims=True)
    step = step.astype(BF16).astype(F32)
    spread = jnp.concatenate(
        [jnp.broadcast_to(step[:, c * cols : c * cols + cols], (16, cols)) for c in range(3)], axis=0
    )
    spread = jnp.where(same, spread, 0.0).astype(BF16)
    for g in range(groups):
        at = slice(16 * g, 16 * g + 16)
        term = mm(spread, basis[:, at, :].reshape(cols, cols))
        for c in range(3):
            out[c, at, :] = own[c, at, :] + term[16 * c : 16 * c + 16, :]
    for copy in halo + fix:
        copy.wait_send()
    for c in range(3):
        for copy in tan[c] + res[c]:
            copy.wait_send()
    whole(sum1_dst, 0).wait_send()
    whole(sum2_dst, 1).wait_send()


def body(nrow, ncol, *args):
    vm = pltpu.VMEM
    dma = pltpu.SemaphoreType.DMA
    return pl.pallas_call(
        functools.partial(kernel, nrow, ncol),
        out_shape=vm((3, 128, 256), F32),
        in_specs=[pl.BlockSpec(memory_space=pltpu.HBM)] * 9,
        out_specs=pl.BlockSpec(memory_space=vm),
        scratch_shapes=[
            vm((3, 144, 256), F32),
            vm((3, 128, 256), F32),
            vm((128, 256), jnp.int32),
            vm((128, 256), jnp.int32),
            pltpu.SMEM((8,), F32),
            pltpu.SMEM((1, 1), jnp.int32),
            vm((3, 256, 256), BF16),
            vm((16, 128, 256), BF16),
            vm((48, 48), F32),
            vm((128, 256), F32),
            vm((3, 256, 256), BF16),
            vm((3, 128, 256), F32),
            vm((2, 8, 256), F32),
            vm((2, 8, 256), F32),
            vm((16, 128), F32),
            vm((16, 128), F32),
            vm((2, 3, 64, 256), BF16),
            vm((2, 3, 64, 256), BF16),
            vm((1, 128), F32),
            vm((ncol - 1, 1, 128), F32),
            vm((1, 128), F32),
            vm((nrow - 1, 1, 128), F32),
            vm((128, 768), BF16),
            vm((3, 16, 256), BF16),
            vm((3, 128, 256), BF16),
            vm((2, 24, 128), F32),
            vm((2, 24, 128), F32),
            vm((2, 16, 256), F32),
            vm((2, 128, 256), BF16),
            dma((9,)),
            dma((4,)),
            dma((4,)),
            dma((3, 2)),
            dma((3, 2)),
            dma((2,)),
            dma((2,)),
            dma((3, 2)),
            dma((3, 2)),
            dma((2,)),
            dma((2,)),
            pltpu.SemaphoreType.REGULAR((3,)),
        ],
        compiler_params=pltpu.CompilerParams(
            collective_id=0, has_side_effects=True, vmem_limit_bytes=56 * 1024 * 1024
        ),
        name="schwarz",
    )(*args)


def solution(mesh):
    placed = (
        P(None, "prow", "pcol"),
        P(None, "prow", "pcol"),
        P("prow", "pcol"),
        P("prow", "pcol"),
        P(),
        P("prow", "pcol"),
        P("prow", "pcol", None, None, None),
        P(None, "prow", "pcol"),
        P(),
    )
    return jax.shard_map(
        functools.partial(body, mesh.shape["prow"], mesh.shape["pcol"]),
        mesh=mesh,
        in_specs=placed,
        out_specs=P(None, "prow", "pcol"),
        check_vma=False,
    )
```

```python
import functools

import jax
import jax.numpy as jnp
from jax import lax
from jax.experimental import pallas as pl
from jax.experimental.pallas import tpu as pltpu
from jax.sharding import PartitionSpec as P

MESH = pl.DeviceIdType.MESH
F32 = jnp.float32
BF16 = jnp.bfloat16
NT = (((1,), (1,)), ((), ()))
TN = (((0,), (0,)), ((), ()))


def iota(shape, dim):
    return lax.broadcasted_iota(jnp.int32, shape, dim)


def mm(a, b, dims=(((1,), (0,)), ((), ()))):
    return lax.dot_general(a, b, dims, preferred_element_type=F32)


def ones_where(cond):
    return jnp.where(cond, 1.0, 0.0).astype(BF16)


def ring(k, n):
    return min(k % n, n - k % n)


def near_set(xs, ys, reach):
    found = [(dx, dy) for dx in range(xs) for dy in range(ys) if 0 < ring(dx, xs) + ring(dy, ys) <= reach]
    return sorted(found, key=lambda o: (ring(o[0], xs) + ring(o[1], ys), o))


def row_plan(xs, ys):
    def shift(p, q):
        return ((p[0] + q[0]) % xs, (p[1] + q[1]) % ys)

    def offsets(pairs):
        return {shift((0, 0), p) for p in pairs} - {(0, 0)}

    first = offsets([(1, 0), (0, -1)])
    known, levels = set(first), []
    while len(known) < xs * ys - 1:
        if not levels:
            told = first
        elif len(levels) == 1:
            told = set(known)
        else:
            told = offsets([(0, 2), (0, -2)])
        assert told <= known
        back = offsets([(-p[0], -p[1]) for p in told])
        known = known | back | {shift(p, q) for p in back for q in known}
        known.discard((0, 0))
        levels.append(sorted(told))
    return sorted(first), levels


def line_plan(n):
    first = [k for k in range(1, n) if ring(k, n) <= 2]
    levels, reach = [], 2
    while reach < n // 2:
        levels.append(sorted({reach, n - reach}))
        reach *= 2
    return first, levels


def kernel(
    nrow,
    ncol,
    dir_hbm,
    state_hbm,
    mat_hbm,
    trim_hbm,
    moduli_hbm,
    band_hbm,
    blocks_hbm,
    basis_hbm,
    inv_hbm,
    out,
    dpad,
    state,
    mat,
    trim,
    moduli,
    band,
    blk,
    basis,
    inv,
    coef,
    wide,
    own,
    row_src,
    row_dst,
    col_src,
    col_dst,
    res_src,
    res_dst,
    sum1_src,
    sum1_dst,
    sum2_src,
    sum2_dst,
    irep,
    place,
    inner,
    fix_src,
    fix_dst,
    edge_rows,
    rim_src,
    rim_dst,
    load_sem,
    halo_ssem,
    halo_rsem,
    tan_ssem,
    tan_rsem,
    fix_ssem,
    fix_rsem,
    rim_ssem,
    rim_rsem,
    res_ssem,
    res_rsem,
    sum_ssem,
    sum_rsem,
    entry_sem,
):
    d = lax.axis_index("prow")
    e = lax.axis_index("pcol")

    def col_at(k):
        return (d, lax.rem(e + k % ncol, ncol))

    xs, ys = 4, nrow // 4
    x = lax.rem(d, xs)
    y = d // xs

    def row_at(offset):
        dx, dy = offset
        return (lax.rem(y + dy, ys) * xs + lax.rem(x + dx, xs), e)

    up, down = (lax.rem(d + nrow - 1, nrow), e), (lax.rem(d + 1, nrow), e)
    left, right = col_at(-1), col_at(1)
    rows, cols = 128, 256
    groups = rows // 16

    def signal(sem, to):
        pl.semaphore_signal(sem, inc=1, device_id=to, device_id_type=MESH)

    row_first, row_levels = row_plan(xs, ys)
    col_first, col_levels = line_plan(ncol)

    def load(src, dst, i):
        copy = pltpu.make_async_copy(src, dst, load_sem.at[i])
        copy.start()
        return copy

    l_dir = load(dir_hbm, dpad.at[:, pl.ds(8, rows), :], 0)
    barrier = pltpu.get_barrier_semaphore()
    for dx, dy in row_first:
        signal(barrier, row_at((-dx % xs, -dy % ys)))
    for k in col_first:
        signal(barrier, col_at(-k))
    l_state = load(state_hbm, state, 1)
    l_mat = load(mat_hbm, mat, 2)
    l_trim = load(trim_hbm, trim, 3)
    l_mod = load(moduli_hbm, moduli, 4)
    last = rows - 16
    l_ends = [load(basis_hbm.at[:, pl.ds(r, 16)], basis.at[:, pl.ds(r, 16)], i) for r, i in ((0, 9), (last, 10))]
    l_basis = load(basis_hbm.at[:, pl.ds(16, rows - 32)], basis.at[:, pl.ds(16, rows - 32)], 5)
    l_blk = load(blocks_hbm.at[0, 0], blk, 6)
    l_band = load(band_hbm, band, 7)
    l_inv = load(inv_hbm, inv, 8)

    def send(src, dst, ssem, rsem, to):
        copy = pltpu.make_async_remote_copy(
            src_ref=src, dst_ref=dst, send_sem=ssem, recv_sem=rsem, device_id=to, device_id_type=MESH
        )
        copy.start()
        return copy

    def tell(level):
        count = 0
        for levels, at in ((row_levels, row_at), (col_levels, col_at)):
            if level < len(levels):
                for k in levels[level]:
                    signal(entry_sem.at[level], at(k))
                count += len(levels[level])
        return count

    def hear(level, count):
        if count:
            pl.semaphore_wait(entry_sem.at[level], count)

    r16 = iota((16, cols), 0)
    c16 = iota((16, cols), 1)
    l_dir.wait()
    row_src[...] = jnp.zeros_like(row_src)
    edge_cols = jnp.zeros((16, rows), F32)
    for c in range(3):
        row_src[0, c : c + 1, :] = dpad[c, 8:9, :]
        row_src[1, c : c + 1, :] = dpad[c, 7 + rows : 8 + rows, :]
        pick = ones_where(((r16 == c) & (c16 == 0)) | ((r16 == 8 + c) & (c16 == cols - 1)))
        place[c] = pick
        edge_cols = edge_cols + mm(pick, dpad[c, 8 : 8 + rows, :].astype(BF16), NT)
    col_src[...] = edge_cols
    l_state.wait()
    l_mat.wait()
    l_trim.wait()
    l_mod.wait()
    for g in range(groups):
        at = slice(16 * g, 16 * g + 16)
        s0, s1, s2 = state[0, at, :], state[1, at, :], state[2, at, :]
        stretch = 1.0 + 0.3 * (s0 * s0 + s1 * s1 + s2 * s2)
        which = mat[at, :]
        table = jnp.full((16, cols), moduli[0], F32)
        for entry in range(1, 8):
            table = jnp.where(which == entry, moduli[entry], table)
        coef[at, :] = table * (stretch + 1.0 / stretch) * (0.25 + 0.75 * trim[at, :].astype(F32))

    for copy in l_ends:
        copy.wait()
    for i in range(2):
        edge = coef[(rows - 1) * i : (rows - 1) * i + 1, :]
        for k in range(16):
            line = basis[k, last * i : last * i + 16, :].astype(F32)[15 * i : 15 * i + 1, :]
            edge_rows[i, k : k + 1, :] = line * edge
        rim_src[i, 0:16, :] = jnp.concatenate([row_src[1 * i], jnp.zeros((8, cols), F32)], axis=0).astype(BF16)
        rim_src[i, 16:32, :] = edge_rows[i].astype(BF16)
    pl.semaphore_wait(barrier, len(row_first) + len(col_first))
    halo = [
        send(col_src.at[pl.ds(0, 8)], col_dst.at[pl.ds(8, 8)], halo_ssem.at[2], halo_rsem.at[2], left),
        send(col_src.at[pl.ds(8, 8)], col_dst.at[pl.ds(0, 8)], halo_ssem.at[3], halo_rsem.at[3], right),
    ]
    told = tell(0)

    rim_up = pltpu.make_async_remote_copy(
        src_ref=rim_src.at[0], dst_ref=rim_dst.at[0], send_sem=rim_ssem.at[0], recv_sem=rim_rsem.at[0],
        device_id=row_at((0, ys - 1)), device_id_type=MESH,
    )

    @pl.when(x == 0)
    def _():
        rim_up.start()

    rim_right = send(rim_src.at[1], rim_dst.at[1], rim_ssem.at[1], rim_rsem.at[1], row_at((1, 0)))

    lane = iota((16, cols), 1)
    side = iota((16, cols), 0)
    zero_row = jnp.zeros((1, cols), F32)
    for c in range(3):
        dpad[c, 7:8, :] = zero_row
        dpad[c, 8 + rows : 9 + rows, :] = zero_row
        for g in range(groups):
            r0 = 8 + 16 * g
            at = slice(16 * g, 16 * g + 16)
            centre = dpad[c, r0 : r0 + 16, :]
            beside = dpad[c, r0 - 1 : r0 + 15, :] + dpad[c, r0 + 1 : r0 + 17, :]
            beside = beside + jnp.where(lane == 0, 0.0, pltpu.roll(centre, 1, 1))
            beside = beside + jnp.where(lane == cols - 1, 0.0, pltpu.roll(centre, cols - 1, 1))
            coupled = dpad[(c + 1) % 3, r0 : r0 + 16, :]
            value = coef[at, :] * (5.0 * centre - beside + 0.5 * coupled)
            own[c, at, :] = value
            inner[c, at, :] = value.astype(BF16)

    coef_high = coef[...].astype(BF16)
    coef_low = (coef[...] - coef_high.astype(F32)).astype(BF16)
    both = ones_where(((r16 < 8) & (c16 == 0)) | ((r16 >= 8) & (c16 == cols - 1)))
    coef_cols = mm(both, coef_high, NT) + mm(both, coef_low, NT)

    hear(0, told)
    told = tell(1)
    halo += [
        send(row_src.at[0], row_dst.at[1], halo_ssem.at[0], halo_rsem.at[0], up),
        send(row_src.at[1], row_dst.at[0], halo_ssem.at[1], halo_rsem.at[1], down),
    ]
    tan = []
    for c in range(3):
        tan.append(
            (
                send(inner.at[c, pl.ds(0, 64)], wide.at[c, pl.ds(192, 64)], tan_ssem.at[c, 0], tan_rsem.at[c, 0], up),
                send(inner.at[c, pl.ds(64, 64)], wide.at[c, pl.ds(0, 64)], tan_ssem.at[c, 1], tan_rsem.at[c, 1], down),
            )
        )

    l_basis.wait()
    r48 = iota((48, cols), 0)
    c48 = iota((48, cols), 1)
    same = (r48 % 16) == (c48 % 16)
    re = iota((cols, 128), 0)
    ce = iota((cols, 128), 1)
    fold = ones_where(((ce % 16) == (re // 16)) & (ce < 96))
    rp = iota((48, 128), 0)
    cp = iota((48, 128), 1)
    acc = jnp.zeros((48, cols), F32)
    for g in range(groups):
        own_rows = inner[:, 16 * g : 16 * g + 16, :].reshape(48, cols)
        functions = basis[:, 16 * g : 16 * g + 16, :].reshape(cols, cols)
        acc = acc + mm(own_rows, functions, NT)
    acc = jnp.where(same, acc, 0.0)
    high = acc.astype(BF16)
    low = (acc - high.astype(F32)).astype(BF16)
    part = mm(high, fold) + mm(low, fold)
    part = jnp.where((((cp // 16) % 3) == (rp // 16)) & (cp < 96), part, 0.0)
    sum1_src[...] = jnp.sum(part, axis=0, keepdims=True)

    rb = iota((cols, cols), 0)
    cb = iota((cols, cols), 1)
    ends = ones_where(((rb == 0) & (cb < 128)) | ((rb == cols - 1) & (cb >= 128)))
    lb = iota((rows, cols), 1)
    edge_basis = jnp.zeros((rows, cols), F32)
    for k in range(16):
        edge_basis = jnp.where(lb % 16 == k, mm(basis[k], ends), edge_basis)
    edge_basis = edge_basis.astype(BF16)

    halo[0].wait_recv()
    halo[1].wait_recv()
    half = iota((16, rows), 0)
    keep = ((half < 8) & (e > 0)) | ((half >= 8) & (e < ncol - 1))
    shares = -coef_cols * jnp.where(keep, col_dst[...], 0.0)
    shares_low = shares.astype(BF16)
    rh = iota((16, 128), 0)
    ch = iota((16, 128), 1)
    part = jnp.where(rh < 8, mm(shares_low, edge_basis[:, 0:128]), mm(shares_low, edge_basis[:, 128:256]))
    part = jnp.where(((ch // 16) % 3 == rh % 8) & (rh % 8 < 3) & (ch < 96), part, 0.0)
    sum1_src[...] = sum1_src[...] + jnp.sum(part, axis=0, keepdims=True)

    for i in range(2):
        fix_src[i, 0:16, :] = shares
        edge = coef[(rows - 1) * i : (rows - 1) * i + 1, :]
        fix_src[i, 16:24, :] = jnp.concatenate(
            [jnp.broadcast_to(edge[:, 0:128], (4, 128)), jnp.broadcast_to(edge[:, 128:256], (4, 128))], axis=0
        )
    fix = [
        send(fix_src.at[0], fix_dst.at[1], fix_ssem.at[0], fix_rsem.at[0], up),
        send(fix_src.at[1], fix_dst.at[0], fix_ssem.at[1], fix_rsem.at[1], down),
    ]

    @pl.when(x == 0)
    def _():
        rim_up.wait_recv()

    @pl.when(x != 0)
    def _():
        rim_dst[0] = rim_src[0]

    rim_right.wait_recv()
    upper = rim_dst[1]
    lower = rim_dst[0]
    values = jnp.concatenate([upper[0:16, :], lower[0:16, :]], axis=1)
    edge = jnp.concatenate([lower[16:32, :], upper[16:32, :]], axis=1)
    edge = jnp.concatenate([edge] * 6 + [jnp.zeros((32, 2 * cols), BF16)], axis=0)
    inside = (x > 0) | (y < ys - 1)
    part = jnp.where(((ch // 16) % 3 == rh) & (ch < 96) & inside, mm(values, edge, NT), 0.0)
    sum1_src[...] = sum1_src[...] - jnp.sum(part, axis=0, keepdims=True)
    hear(1, told)
    told = tell(2)
    for k in sorted(range(1, ncol), key=lambda k: (-ring(k, ncol), k)):
        send(sum1_src, sum1_dst.at[k - 1], sum_ssem.at[0], sum_rsem.at[0], col_at(k))

    l_blk.wait()
    l_band.wait()
    width = band[0, 0]
    for i in range(8):
        t = iota((32, 256), 0) + 32 * i
        s = iota((32, 256), 1)
        keep = jnp.abs(t - s) <= width
        keep = keep & ((s >= 64) | (d > 0)) & ((s < 192) | (d < nrow - 1))
        keep = keep & ((t >= 64) | (d > 0)) & ((t < 192) | (d < nrow - 1))
        factor = 0.5 if (i < 2 or i >= 6) else 1.0
        factor = jnp.where(keep, factor, 0.0).astype(BF16)
        for c in range(3):
            blk[c, 32 * i : 32 * i + 32, :] = blk[c, 32 * i : 32 * i + 32, :] * factor

    l_inv.wait()
    inv_high = inv[...].astype(BF16)
    inv_low = (inv[...] - inv_high.astype(F32)).astype(BF16)
    repeat = ones_where((iota((48, 768), 1) // 16) == iota((48, 768), 0))
    irep[0:48, :] = mm(inv_high, repeat, TN).astype(BF16)
    irep[48:96, :] = mm(inv_low, repeat, TN).astype(BF16)
    irep[96:128, :] = jnp.zeros((32, 768), BF16)

    halo[2].wait_recv()
    halo[3].wait_recv()
    above = jnp.where(d > 0, row_dst[0], 0.0) * -coef[0:1, :]
    below = jnp.where(d < nrow - 1, row_dst[1], 0.0) * -coef[rows - 1 : rows, :]
    for c in range(3):
        sides = mm(shares_low, place[c], TN)
        for g in range(groups):
            at = slice(16 * g, 16 * g + 16)
            value = own[c, at, :] + sides[at, :]
            if g == 0:
                value = value + jnp.where(side == 0, above[c : c + 1, :], 0.0)
            if g == groups - 1:
                value = value + jnp.where(side == 15, below[c : c + 1, :], 0.0)
            wide[c, 64 + 16 * g : 80 + 16 * g, :] = value.astype(BF16)

    def whole(buf, stage):
        return pltpu.make_async_remote_copy(
            src_ref=buf, dst_ref=buf, send_sem=sum_ssem.at[stage], recv_sem=sum_rsem.at[stage],
            device_id=right, device_id_type=MESH,
        )

    res = []

    def local(c):
        for copy in tan[c]:
            copy.wait_recv()
        if c == 0:
            for copy in fix:
                copy.wait_recv()
        for i in range(2):
            sides = mm(fix_dst[i, 0:16, :].astype(BF16), place[c], TN)
            edge = jnp.concatenate([fix_dst[i, 16:17, :], fix_dst[i, 20:21, :]], axis=1)
            beyond = dpad[c, 8:9, :] if i == 0 else dpad[c, 7 + rows : 8 + rows, :]
            for j in range(4):
                to = slice(192 * i + 16 * j, 192 * i + 16 * j + 16)
                lines = slice(64 * (1 - i) + 16 * j, 64 * (1 - i) + 16 * j + 16)
                value = wide[c, to, :].astype(F32) + sides[lines, :]
                if j == (3 if i == 0 else 0):
                    value = value - jnp.where(side == (15 if i == 0 else 0), edge * beyond, 0.0)
                wide[c, to, :] = value.astype(BF16)
        vec = wide[c]
        margins = mm(jnp.concatenate([blk[c, 0:64, :], blk[c, 192:256, :]], axis=0), vec)
        res_src[0, c] = margins[0:64, :].astype(BF16)
        res_src[1, c] = margins[64:128, :].astype(BF16)
        res.append(
            (
                send(res_src.at[0, c], res_dst.at[1, c], res_ssem.at[c, 0], res_rsem.at[c, 0], up),
                send(res_src.at[1, c], res_dst.at[0, c], res_ssem.at[c, 1], res_rsem.at[c, 1], down),
            )
        )

    local(0)

    whole(sum1_dst, 0).wait_recv()
    sum2_src[...] = sum1_src[...] + jnp.sum(sum1_dst[...], axis=0)
    hear(2, told)
    for offset in reversed(near_set(xs, ys, nrow)):
        slot = offset[1] * xs + offset[0] - 1
        send(sum2_src, sum2_dst.at[slot], sum_ssem.at[1], sum_rsem.at[1], row_at(offset))

    local(1)
    local(2)

    for c in range(3):
        own[c] = mm(blk[c, 64:192, :], wide[c])
    for c in range(3):
        for copy in res[c]:
            copy.wait_recv()
        own[c, 0:64, :] = own[c, 0:64, :] + res_dst[0, c].astype(F32)
        own[c, 64:128, :] = own[c, 64:128, :] + res_dst[1, c].astype(F32)

    whole(sum2_dst, 1).wait_recv()
    total = sum2_src[...] + jnp.sum(sum2_dst[...], axis=0)
    total = jnp.broadcast_to(total, (16, 128))
    high = total.astype(BF16).astype(F32)
    mid = (total - high).astype(BF16).astype(F32)
    low = total - high - mid
    rt = iota((16, 128), 0)
    split = jnp.where(rt == 0, high, jnp.where(rt == 1, mid, jnp.where(rt == 2, low, 0.0))).astype(BF16)
    step = jnp.sum(mm(split, irep[...]), axis=0, keepdims=True)
    step = step.astype(BF16).astype(F32)
    spread = jnp.concatenate(
        [jnp.broadcast_to(step[:, c * cols : c * cols + cols], (16, cols)) for c in range(3)], axis=0
    )
    spread = jnp.where(same, spread, 0.0).astype(BF16)
    for g in range(groups):
        at = slice(16 * g, 16 * g + 16)
        term = mm(spread, basis[:, at, :].reshape(cols, cols))
        for c in range(3):
            out[c, at, :] = own[c, at, :] + term[16 * c : 16 * c + 16, :]
    for copy in halo + fix + [rim_right]:
        copy.wait_send()

    @pl.when(x == 0)
    def _():
        rim_up.wait_send()

    for c in range(3):
        for copy in tan[c] + res[c]:
            copy.wait_send()
    whole(sum1_dst, 0).wait_send()
    whole(sum2_dst, 1).wait_send()


def body(nrow, ncol, *args):
    vm = pltpu.VMEM
    dma = pltpu.SemaphoreType.DMA
    return pl.pallas_call(
        functools.partial(kernel, nrow, ncol),
        out_shape=vm((3, 128, 256), F32),
        in_specs=[pl.BlockSpec(memory_space=pltpu.HBM)] * 9,
        out_specs=pl.BlockSpec(memory_space=vm),
        scratch_shapes=[
            vm((3, 144, 256), F32),
            vm((3, 128, 256), F32),
            vm((128, 256), jnp.int32),
            vm((128, 256), jnp.int32),
            pltpu.SMEM((8,), F32),
            pltpu.SMEM((1, 1), jnp.int32),
            vm((3, 256, 256), BF16),
            vm((16, 128, 256), BF16),
            vm((48, 48), F32),
            vm((128, 256), F32),
            vm((3, 256, 256), BF16),
            vm((3, 128, 256), F32),
            vm((2, 8, 256), F32),
            vm((2, 8, 256), F32),
            vm((16, 128), F32),
            vm((16, 128), F32),
            vm((2, 3, 64, 256), BF16),
            vm((2, 3, 64, 256), BF16),
            vm((1, 128), F32),
            vm((ncol - 1, 1, 128), F32),
            vm((1, 128), F32),
            vm((nrow - 1, 1, 128), F32),
            vm((128, 768), BF16),
            vm((3, 16, 256), BF16),
            vm((3, 128, 256), BF16),
            vm((2, 24, 128), F32),
            vm((2, 24, 128), F32),
            vm((2, 16, 256), F32),
            vm((2, 32, 256), BF16),
            vm((2, 32, 256), BF16),
            dma((11,)),
            dma((4,)),
            dma((4,)),
            dma((3, 2)),
            dma((3, 2)),
            dma((2,)),
            dma((2,)),
            dma((2,)),
            dma((2,)),
            dma((3, 2)),
            dma((3, 2)),
            dma((2,)),
            dma((2,)),
            pltpu.SemaphoreType.REGULAR((3,)),
        ],
        compiler_params=pltpu.CompilerParams(
            collective_id=0, has_side_effects=True, vmem_limit_bytes=56 * 1024 * 1024
        ),
        name="schwarz",
    )(*args)


def solution(mesh):
    placed = (
        P(None, "prow", "pcol"),
        P(None, "prow", "pcol"),
        P("prow", "pcol"),
        P("prow", "pcol"),
        P(),
        P("prow", "pcol"),
        P("prow", "pcol", None, None, None),
        P(None, "prow", "pcol"),
        P(),
    )
    return jax.shard_map(
        functools.partial(body, mesh.shape["prow"], mesh.shape["pcol"]),
        mesh=mesh,
        in_specs=placed,
        out_specs=P(None, "prow", "pcol"),
        check_vma=False,
    )
```

```python
import functools

import jax
import jax.numpy as jnp
from jax import lax
from jax.experimental import pallas as pl
from jax.experimental.pallas import tpu as pltpu
from jax.sharding import PartitionSpec as P

MESH = pl.DeviceIdType.MESH
F32 = jnp.float32
BF16 = jnp.bfloat16
NT = (((1,), (1,)), ((), ()))
TN = (((0,), (0,)), ((), ()))


def iota(shape, dim):
    return lax.broadcasted_iota(jnp.int32, shape, dim)


def mm(a, b, dims=(((1,), (0,)), ((), ()))):
    return lax.dot_general(a, b, dims, preferred_element_type=F32)


def ones_where(cond):
    return jnp.where(cond, 1.0, 0.0).astype(BF16)


def ring(k, n):
    return min(k % n, n - k % n)


def near_set(xs, ys, reach):
    found = [(dx, dy) for dx in range(xs) for dy in range(ys) if 0 < ring(dx, xs) + ring(dy, ys) <= reach]
    return sorted(found, key=lambda o: (ring(o[0], xs) + ring(o[1], ys), o))


def row_plan(xs, ys):
    def shift(p, q):
        return ((p[0] + q[0]) % xs, (p[1] + q[1]) % ys)

    def offsets(pairs):
        return {shift((0, 0), p) for p in pairs} - {(0, 0)}

    first = offsets([(1, 0), (0, -1)])
    known, levels = set(first), []
    while len(known) < xs * ys - 1:
        if not levels:
            told = first
        elif len(levels) == 1:
            told = set(known)
        else:
            told = offsets([(0, 2), (0, -2)])
        assert told <= known
        back = offsets([(-p[0], -p[1]) for p in told])
        known = known | back | {shift(p, q) for p in back for q in known}
        known.discard((0, 0))
        levels.append(sorted(told))
    return sorted(first), levels


def line_plan(n):
    first = [k for k in range(1, n) if ring(k, n) <= 4]
    levels, reach = [], 4
    while reach < n // 2:
        levels.append(sorted({reach, n - reach}))
        reach *= 2
    return first, levels


def kernel(
    nrow,
    ncol,
    dir_hbm,
    state_hbm,
    mat_hbm,
    trim_hbm,
    moduli_hbm,
    band_hbm,
    blocks_hbm,
    basis_hbm,
    inv_hbm,
    out,
    dpad,
    state,
    mat,
    trim,
    moduli,
    band,
    blk,
    basis,
    inv,
    coef,
    wide,
    own,
    row_src,
    row_dst,
    col_src,
    col_dst,
    res_src,
    res_dst,
    sum1_src,
    sum1_dst,
    sum2_src,
    sum2_dst,
    irep,
    place,
    inner,
    fix_src,
    fix_dst,
    edge_rows,
    rim_src,
    rim_dst,
    load_sem,
    halo_ssem,
    halo_rsem,
    tan_ssem,
    tan_rsem,
    fix_ssem,
    fix_rsem,
    rim_ssem,
    rim_rsem,
    res_ssem,
    res_rsem,
    sum_ssem,
    sum_rsem,
    entry_sem,
):
    d = lax.axis_index("prow")
    e = lax.axis_index("pcol")

    def col_at(k):
        return (d, lax.rem(e + k % ncol, ncol))

    xs, ys = 4, nrow // 4
    x = lax.rem(d, xs)
    y = d // xs

    def row_at(offset):
        dx, dy = offset
        return (lax.rem(y + dy, ys) * xs + lax.rem(x + dx, xs), e)

    up, down = (lax.rem(d + nrow - 1, nrow), e), (lax.rem(d + 1, nrow), e)
    left, right = col_at(-1), col_at(1)
    rows, cols = 128, 256
    groups = rows // 16

    def signal(sem, to):
        pl.semaphore_signal(sem, inc=1, device_id=to, device_id_type=MESH)

    row_first, row_levels = row_plan(xs, ys)
    col_first, col_levels = line_plan(ncol)

    def load(src, dst, i):
        copy = pltpu.make_async_copy(src, dst, load_sem.at[i])
        copy.start()
        return copy

    l_dir = load(dir_hbm, dpad.at[:, pl.ds(8, rows), :], 0)
    barrier = pltpu.get_barrier_semaphore()
    for dx, dy in row_first:
        signal(barrier, row_at((-dx % xs, -dy % ys)))
    for k in col_first:
        signal(barrier, col_at(-k))
    l_state = load(state_hbm, state, 1)
    l_mat = load(mat_hbm, mat, 2)
    l_trim = load(trim_hbm, trim, 3)
    l_mod = load(moduli_hbm, moduli, 4)
    last = rows - 16
    l_ends = [load(basis_hbm.at[:, pl.ds(r, 16)], basis.at[:, pl.ds(r, 16)], i) for r, i in ((0, 9), (last, 10))]
    l_basis = load(basis_hbm.at[:, pl.ds(16, rows - 32)], basis.at[:, pl.ds(16, rows - 32)], 5)
    l_blk = load(blocks_hbm.at[0, 0], blk, 6)
    l_band = load(band_hbm, band, 7)
    l_inv = load(inv_hbm, inv, 8)

    def send(src, dst, ssem, rsem, to):
        copy = pltpu.make_async_remote_copy(
            src_ref=src, dst_ref=dst, send_sem=ssem, recv_sem=rsem, device_id=to, device_id_type=MESH
        )
        copy.start()
        return copy

    def tell(level):
        count = 0
        for levels, at in ((col_levels, col_at), (row_levels, row_at)):
            if level < len(levels):
                for k in levels[level]:
                    signal(entry_sem.at[level], at(k))
                count += len(levels[level])
        return count

    def hear(level, count):
        if count:
            pl.semaphore_wait(entry_sem.at[level], count)

    r16 = iota((16, cols), 0)
    c16 = iota((16, cols), 1)
    l_dir.wait()
    row_src[...] = jnp.zeros_like(row_src)
    edge_cols = jnp.zeros((16, rows), F32)
    for c in range(3):
        row_src[0, c : c + 1, :] = dpad[c, 8:9, :]
        row_src[1, c : c + 1, :] = dpad[c, 7 + rows : 8 + rows, :]
        pick = ones_where(((r16 == c) & (c16 == 0)) | ((r16 == 8 + c) & (c16 == cols - 1)))
        place[c] = pick
        edge_cols = edge_cols + mm(pick, dpad[c, 8 : 8 + rows, :].astype(BF16), NT)
    col_src[...] = edge_cols
    l_state.wait()
    l_mat.wait()
    l_trim.wait()
    l_mod.wait()
    for g in range(groups):
        at = slice(16 * g, 16 * g + 16)
        s0, s1, s2 = state[0, at, :], state[1, at, :], state[2, at, :]
        stretch = 1.0 + 0.3 * (s0 * s0 + s1 * s1 + s2 * s2)
        which = mat[at, :]
        table = jnp.full((16, cols), moduli[0], F32)
        for entry in range(1, 8):
            table = jnp.where(which == entry, moduli[entry], table)
        coef[at, :] = table * (stretch + 1.0 / stretch) * (0.25 + 0.75 * trim[at, :].astype(F32))

    for copy in l_ends:
        copy.wait()
    for i in range(2):
        edge = coef[(rows - 1) * i : (rows - 1) * i + 1, :]
        for k in range(16):
            line = basis[k, last * i : last * i + 16, :].astype(F32)[15 * i : 15 * i + 1, :]
            edge_rows[i, k : k + 1, :] = line * edge
        rim_src[i, 0:16, :] = jnp.concatenate([row_src[1 * i], jnp.zeros((8, cols), F32)], axis=0).astype(BF16)
        rim_src[i, 16:32, :] = edge_rows[i].astype(BF16)
    lane = iota((16, cols), 1)
    side = iota((16, cols), 0)
    zero_row = jnp.zeros((1, cols), F32)
    for c in range(3):
        dpad[c, 7:8, :] = zero_row
        dpad[c, 8 + rows : 9 + rows, :] = zero_row
        for g in range(groups):
            r0 = 8 + 16 * g
            at = slice(16 * g, 16 * g + 16)
            centre = dpad[c, r0 : r0 + 16, :]
            beside = dpad[c, r0 - 1 : r0 + 15, :] + dpad[c, r0 + 1 : r0 + 17, :]
            beside = beside + jnp.where(lane == 0, 0.0, pltpu.roll(centre, 1, 1))
            beside = beside + jnp.where(lane == cols - 1, 0.0, pltpu.roll(centre, cols - 1, 1))
            coupled = dpad[(c + 1) % 3, r0 : r0 + 16, :]
            value = coef[at, :] * (5.0 * centre - beside + 0.5 * coupled)
            own[c, at, :] = value
            inner[c, at, :] = value.astype(BF16)

    coef_high = coef[...].astype(BF16)
    coef_low = (coef[...] - coef_high.astype(F32)).astype(BF16)
    both = ones_where(((r16 < 8) & (c16 == 0)) | ((r16 >= 8) & (c16 == cols - 1)))
    coef_cols = mm(both, coef_high, NT) + mm(both, coef_low, NT)

    pl.semaphore_wait(barrier, len(row_first) + len(col_first))
    told = tell(0)
    halo = [
        send(col_src.at[pl.ds(0, 8)], col_dst.at[pl.ds(8, 8)], halo_ssem.at[2], halo_rsem.at[2], left),
        send(col_src.at[pl.ds(8, 8)], col_dst.at[pl.ds(0, 8)], halo_ssem.at[3], halo_rsem.at[3], right),
    ]

    @pl.when(x != 0)
    def _():
        rim_dst[0] = rim_src[0]

    rim_up = pltpu.make_async_remote_copy(
        src_ref=rim_src.at[0], dst_ref=rim_dst.at[0], send_sem=rim_ssem.at[0], recv_sem=rim_rsem.at[0],
        device_id=row_at((0, ys - 1)), device_id_type=MESH,
    )

    @pl.when(x == 0)
    def _():
        rim_up.start()

    rim_right = send(rim_src.at[1], rim_dst.at[1], rim_ssem.at[1], rim_rsem.at[1], row_at((1, 0)))

    l_basis.wait()
    r48 = iota((48, cols), 0)
    c48 = iota((48, cols), 1)
    same = (r48 % 16) == (c48 % 16)
    re = iota((cols, 128), 0)
    ce = iota((cols, 128), 1)
    fold = ones_where(((ce % 16) == (re // 16)) & (ce < 96))
    rp = iota((48, 128), 0)
    cp = iota((48, 128), 1)
    acc = jnp.zeros((48, cols), F32)
    for g in range(groups):
        own_rows = inner[:, 16 * g : 16 * g + 16, :].reshape(48, cols)
        functions = basis[:, 16 * g : 16 * g + 16, :].reshape(cols, cols)
        acc = acc + mm(own_rows, functions, NT)
    acc = jnp.where(same, acc, 0.0)
    high = acc.astype(BF16)
    low = (acc - high.astype(F32)).astype(BF16)
    part = mm(high, fold) + mm(low, fold)
    part = jnp.where((((cp // 16) % 3) == (rp // 16)) & (cp < 96), part, 0.0)
    sum1_src[...] = jnp.sum(part, axis=0, keepdims=True)

    rb = iota((32, cols), 0)
    cb = iota((32, cols), 1)
    edge_basis = jnp.zeros((32, rows), F32)
    for k in range(16):
        ends = ones_where(((rb == k) & (cb == 0)) | ((rb == 16 + k) & (cb == cols - 1)))
        edge_basis = edge_basis + mm(ends, basis[k], NT)
    edge_basis = edge_basis.astype(BF16)
    blank = jnp.zeros((32, rows), BF16)
    first_basis = jnp.concatenate([edge_basis[0:16, :]] * 6 + [blank], axis=0)
    last_basis = jnp.concatenate([edge_basis[16:32, :]] * 6 + [blank], axis=0)

    hear(0, told)
    told = tell(1)
    halo += [
        send(row_src.at[0], row_dst.at[1], halo_ssem.at[0], halo_rsem.at[0], up),
        send(row_src.at[1], row_dst.at[0], halo_ssem.at[1], halo_rsem.at[1], down),
    ]
    tan = []
    for c in range(3):
        tan.append(
            (
                send(inner.at[c, pl.ds(0, 64)], wide.at[c, pl.ds(192, 64)], tan_ssem.at[c, 0], tan_rsem.at[c, 0], up),
                send(inner.at[c, pl.ds(64, 64)], wide.at[c, pl.ds(0, 64)], tan_ssem.at[c, 1], tan_rsem.at[c, 1], down),
            )
        )

    halo[0].wait_recv()
    halo[1].wait_recv()
    half = iota((16, rows), 0)
    keep = ((half < 8) & (e > 0)) | ((half >= 8) & (e < ncol - 1))
    shares = -coef_cols * jnp.where(keep, col_dst[...], 0.0)
    shares_low = shares.astype(BF16)
    rh = iota((16, 128), 0)
    ch = iota((16, 128), 1)

    for i in range(2):
        fix_src[i, 0:16, :] = shares
        edge = coef[(rows - 1) * i : (rows - 1) * i + 1, :]
        fix_src[i, 16:24, :] = jnp.concatenate(
            [jnp.broadcast_to(edge[:, 0:128], (4, 128)), jnp.broadcast_to(edge[:, 128:256], (4, 128))], axis=0
        )
    fix = [
        send(fix_src.at[0], fix_dst.at[1], fix_ssem.at[0], fix_rsem.at[0], up),
        send(fix_src.at[1], fix_dst.at[0], fix_ssem.at[1], fix_rsem.at[1], down),
    ]

    @pl.when(x == 0)
    def _():
        rim_up.wait_recv()

    rim_right.wait_recv()
    upper = rim_dst[1]
    lower = rim_dst[0]
    values = jnp.concatenate([upper[0:16, :], lower[0:16, :]], axis=1)
    edge = jnp.concatenate([lower[16:32, :], upper[16:32, :]], axis=1)
    edge = jnp.concatenate([edge] * 6 + [jnp.zeros((32, 2 * cols), BF16)], axis=0)
    inside = (x > 0) | (y < ys - 1)
    across = jnp.where(inside, mm(values, edge, NT), 0.0)
    part = jnp.where(rh < 8, mm(shares_low, first_basis, NT) - across, mm(shares_low, last_basis, NT))
    part = jnp.where(((ch // 16) % 3 == rh % 8) & (rh % 8 < 3) & (ch < 96), part, 0.0)
    sum1_src[...] = sum1_src[...] + jnp.sum(part, axis=0, keepdims=True)
    for k in sorted(range(1, ncol), key=lambda k: (-ring(k, ncol), k)):
        send(sum1_src, sum1_dst.at[k - 1], sum_ssem.at[0], sum_rsem.at[0], col_at(k))
    hear(1, told)
    told = tell(2)

    l_blk.wait()
    l_band.wait()
    width = band[0, 0]
    for i in range(8):
        t = iota((32, 256), 0) + 32 * i
        s = iota((32, 256), 1)
        keep = jnp.abs(t - s) <= width
        keep = keep & ((s >= 64) | (d > 0)) & ((s < 192) | (d < nrow - 1))
        keep = keep & ((t >= 64) | (d > 0)) & ((t < 192) | (d < nrow - 1))
        factor = 0.5 if (i < 2 or i >= 6) else 1.0
        factor = jnp.where(keep, factor, 0.0).astype(BF16)
        for c in range(3):
            blk[c, 32 * i : 32 * i + 32, :] = blk[c, 32 * i : 32 * i + 32, :] * factor

    l_inv.wait()
    inv_high = inv[...].astype(BF16)
    inv_low = (inv[...] - inv_high.astype(F32)).astype(BF16)
    repeat = ones_where((iota((48, 768), 1) // 16) == iota((48, 768), 0))
    irep[0:48, :] = mm(inv_high, repeat, TN).astype(BF16)
    irep[48:96, :] = mm(inv_low, repeat, TN).astype(BF16)
    irep[96:128, :] = jnp.zeros((32, 768), BF16)

    halo[2].wait_recv()
    halo[3].wait_recv()
    above = jnp.where(d > 0, row_dst[0], 0.0) * -coef[0:1, :]
    below = jnp.where(d < nrow - 1, row_dst[1], 0.0) * -coef[rows - 1 : rows, :]
    for c in range(3):
        sides = mm(shares_low, place[c], TN)
        for g in range(groups):
            at = slice(16 * g, 16 * g + 16)
            value = own[c, at, :] + sides[at, :]
            if g == 0:
                value = value + jnp.where(side == 0, above[c : c + 1, :], 0.0)
            if g == groups - 1:
                value = value + jnp.where(side == 15, below[c : c + 1, :], 0.0)
            wide[c, 64 + 16 * g : 80 + 16 * g, :] = value.astype(BF16)

    def whole(buf, stage):
        return pltpu.make_async_remote_copy(
            src_ref=buf, dst_ref=buf, send_sem=sum_ssem.at[stage], recv_sem=sum_rsem.at[stage],
            device_id=right, device_id_type=MESH,
        )

    res = []

    def local(c):
        for copy in tan[c]:
            copy.wait_recv()
        if c == 0:
            for copy in fix:
                copy.wait_recv()
        for i in range(2):
            sides = mm(fix_dst[i, 0:16, :].astype(BF16), place[c], TN)
            edge = jnp.concatenate([fix_dst[i, 16:17, :], fix_dst[i, 20:21, :]], axis=1)
            beyond = dpad[c, 8:9, :] if i == 0 else dpad[c, 7 + rows : 8 + rows, :]
            for j in range(4):
                to = slice(192 * i + 16 * j, 192 * i + 16 * j + 16)
                lines = slice(64 * (1 - i) + 16 * j, 64 * (1 - i) + 16 * j + 16)
                value = wide[c, to, :].astype(F32) + sides[lines, :]
                if j == (3 if i == 0 else 0):
                    value = value - jnp.where(side == (15 if i == 0 else 0), edge * beyond, 0.0)
                wide[c, to, :] = value.astype(BF16)
        vec = wide[c]
        margins = mm(jnp.concatenate([blk[c, 0:64, :], blk[c, 192:256, :]], axis=0), vec)
        res_src[0, c] = margins[0:64, :].astype(BF16)
        res_src[1, c] = margins[64:128, :].astype(BF16)
        res.append(
            (
                send(res_src.at[0, c], res_dst.at[1, c], res_ssem.at[c, 0], res_rsem.at[c, 0], up),
                send(res_src.at[1, c], res_dst.at[0, c], res_ssem.at[c, 1], res_rsem.at[c, 1], down),
            )
        )


    whole(sum1_dst, 0).wait_recv()
    sum2_src[...] = sum1_src[...] + jnp.sum(sum1_dst[...], axis=0)
    hear(2, told)
    for offset in reversed(near_set(xs, ys, nrow)):
        slot = offset[1] * xs + offset[0] - 1
        send(sum2_src, sum2_dst.at[slot], sum_ssem.at[1], sum_rsem.at[1], row_at(offset))

    local(0)
    local(1)
    local(2)

    for c in range(3):
        own[c] = mm(blk[c, 64:192, :], wide[c])
    for c in range(3):
        for copy in res[c]:
            copy.wait_recv()
        own[c, 0:64, :] = own[c, 0:64, :] + res_dst[0, c].astype(F32)
        own[c, 64:128, :] = own[c, 64:128, :] + res_dst[1, c].astype(F32)

    whole(sum2_dst, 1).wait_recv()
    total = sum2_src[...] + jnp.sum(sum2_dst[...], axis=0)
    total = jnp.broadcast_to(total, (16, 128))
    high = total.astype(BF16).astype(F32)
    mid = (total - high).astype(BF16).astype(F32)
    low = total - high - mid
    rt = iota((16, 128), 0)
    split = jnp.where(rt == 0, high, jnp.where(rt == 1, mid, jnp.where(rt == 2, low, 0.0))).astype(BF16)
    step = jnp.sum(mm(split, irep[...]), axis=0, keepdims=True)
    step = step.astype(BF16).astype(F32)
    spread = jnp.concatenate(
        [jnp.broadcast_to(step[:, c * cols : c * cols + cols], (16, cols)) for c in range(3)], axis=0
    )
    spread = jnp.where(same, spread, 0.0).astype(BF16)
    for g in range(groups):
        at = slice(16 * g, 16 * g + 16)
        term = mm(spread, basis[:, at, :].reshape(cols, cols))
        for c in range(3):
            out[c, at, :] = own[c, at, :] + term[16 * c : 16 * c + 16, :]
    for copy in halo + fix + [rim_right]:
        copy.wait_send()

    @pl.when(x == 0)
    def _():
        rim_up.wait_send()

    for c in range(3):
        for copy in tan[c] + res[c]:
            copy.wait_send()
    whole(sum1_dst, 0).wait_send()
    whole(sum2_dst, 1).wait_send()


def body(nrow, ncol, *args):
    vm = pltpu.VMEM
    dma = pltpu.SemaphoreType.DMA
    return pl.pallas_call(
        functools.partial(kernel, nrow, ncol),
        out_shape=vm((3, 128, 256), F32),
        in_specs=[pl.BlockSpec(memory_space=pltpu.HBM)] * 9,
        out_specs=pl.BlockSpec(memory_space=vm),
        scratch_shapes=[
            vm((3, 144, 256), F32),
            vm((3, 128, 256), F32),
            vm((128, 256), jnp.int32),
            vm((128, 256), jnp.int32),
            pltpu.SMEM((8,), F32),
            pltpu.SMEM((1, 1), jnp.int32),
            vm((3, 256, 256), BF16),
            vm((16, 128, 256), BF16),
            vm((48, 48), F32),
            vm((128, 256), F32),
            vm((3, 256, 256), BF16),
            vm((3, 128, 256), F32),
            vm((2, 8, 256), F32),
            vm((2, 8, 256), F32),
            vm((16, 128), F32),
            vm((16, 128), F32),
            vm((2, 3, 64, 256), BF16),
            vm((2, 3, 64, 256), BF16),
            vm((1, 128), F32),
            vm((ncol - 1, 1, 128), F32),
            vm((1, 128), F32),
            vm((nrow - 1, 1, 128), F32),
            vm((128, 768), BF16),
            vm((3, 16, 256), BF16),
            vm((3, 128, 256), BF16),
            vm((2, 24, 128), F32),
            vm((2, 24, 128), F32),
            vm((2, 16, 256), F32),
            vm((2, 32, 256), BF16),
            vm((2, 32, 256), BF16),
            dma((11,)),
            dma((4,)),
            dma((4,)),
            dma((3, 2)),
            dma((3, 2)),
            dma((2,)),
            dma((2,)),
            dma((2,)),
            dma((2,)),
            dma((3, 2)),
            dma((3, 2)),
            dma((2,)),
            dma((2,)),
            pltpu.SemaphoreType.REGULAR((3,)),
        ],
        compiler_params=pltpu.CompilerParams(
            collective_id=0, has_side_effects=True, vmem_limit_bytes=56 * 1024 * 1024
        ),
        name="schwarz",
    )(*args)


def solution(mesh):
    placed = (
        P(None, "prow", "pcol"),
        P(None, "prow", "pcol"),
        P("prow", "pcol"),
        P("prow", "pcol"),
        P(),
        P("prow", "pcol"),
        P("prow", "pcol", None, None, None),
        P(None, "prow", "pcol"),
        P(),
    )
    return jax.shard_map(
        functools.partial(body, mesh.shape["prow"], mesh.shape["pcol"]),
        mesh=mesh,
        in_specs=placed,
        out_specs=P(None, "prow", "pcol"),
        check_vma=False,
    )
```

```python
import functools

import jax
import jax.numpy as jnp
from jax import lax
from jax.experimental import pallas as pl
from jax.experimental.pallas import tpu as pltpu
from jax.sharding import PartitionSpec as P

MESH = pl.DeviceIdType.MESH
F32 = jnp.float32
BF16 = jnp.bfloat16
NT = (((1,), (1,)), ((), ()))
TN = (((0,), (0,)), ((), ()))


def iota(shape, dim):
    return lax.broadcasted_iota(jnp.int32, shape, dim)


def mm(a, b, dims=(((1,), (0,)), ((), ()))):
    return lax.dot_general(a, b, dims, preferred_element_type=F32)


def ones_where(cond):
    return jnp.where(cond, 1.0, 0.0).astype(BF16)


def ring(k, n):
    return min(k % n, n - k % n)


def near_set(xs, ys, reach):
    found = [(dx, dy) for dx in range(xs) for dy in range(ys) if 0 < ring(dx, xs) + ring(dy, ys) <= reach]
    return sorted(found, key=lambda o: (ring(o[0], xs) + ring(o[1], ys), o))


def row_plan(xs, ys):
    def shift(p, q):
        return ((p[0] + q[0]) % xs, (p[1] + q[1]) % ys)

    def offsets(pairs):
        return {shift((0, 0), p) for p in pairs} - {(0, 0)}

    first = offsets([(1, 0), (0, -1)])
    known, levels = set(first), []
    while len(known) < xs * ys - 1:
        if not levels:
            told = first
        elif len(levels) == 1:
            told = set(known)
        else:
            told = offsets([(0, 2), (0, -2)])
        assert told <= known
        back = offsets([(-p[0], -p[1]) for p in told])
        known = known | back | {shift(p, q) for p in back for q in known}
        known.discard((0, 0))
        levels.append(sorted(told))
    return sorted(first), levels


def line_plan(n):
    first = [k for k in range(1, n) if ring(k, n) <= 4]
    levels, reach = [], 4
    while reach < n // 2:
        levels.append(sorted({reach, n - reach}))
        reach *= 2
    return first, levels


def kernel(
    nrow,
    ncol,
    dir_hbm,
    state_hbm,
    mat_hbm,
    trim_hbm,
    moduli_hbm,
    band_hbm,
    blocks_hbm,
    basis_hbm,
    inv_hbm,
    out,
    dpad,
    state,
    mat,
    trim,
    moduli,
    band,
    blk,
    basis,
    inv,
    coef,
    wide,
    own,
    row_src,
    row_dst,
    col_src,
    col_dst,
    res_src,
    res_dst,
    sum1_src,
    sum1_dst,
    sum2_src,
    sum2_dst,
    irep,
    place,
    inner,
    fix_src,
    fix_dst,
    edge_rows,
    rim_src,
    rim_dst,
    load_sem,
    halo_ssem,
    halo_rsem,
    tan_ssem,
    tan_rsem,
    fix_ssem,
    fix_rsem,
    rim_ssem,
    rim_rsem,
    res_ssem,
    res_rsem,
    sum_ssem,
    sum_rsem,
    entry_sem,
):
    d = lax.axis_index("prow")
    e = lax.axis_index("pcol")

    def col_at(k):
        return (d, lax.rem(e + k % ncol, ncol))

    xs, ys = 4, nrow // 4
    x = lax.rem(d, xs)
    y = d // xs

    def row_at(offset):
        dx, dy = offset
        return (lax.rem(y + dy, ys) * xs + lax.rem(x + dx, xs), e)

    up, down = (lax.rem(d + nrow - 1, nrow), e), (lax.rem(d + 1, nrow), e)
    left, right = col_at(-1), col_at(1)
    rows, cols = 128, 256
    groups = rows // 16

    def signal(sem, to):
        pl.semaphore_signal(sem, inc=1, device_id=to, device_id_type=MESH)

    row_first, row_levels = row_plan(xs, ys)
    col_first, col_levels = line_plan(ncol)

    def load(src, dst, i):
        copy = pltpu.make_async_copy(src, dst, load_sem.at[i])
        copy.start()
        return copy

    l_dir = load(dir_hbm, dpad.at[:, pl.ds(8, rows), :], 0)
    barrier = pltpu.get_barrier_semaphore()
    for dx, dy in row_first:
        signal(barrier, row_at((-dx % xs, -dy % ys)))
    for k in col_first:
        signal(barrier, col_at(-k))
    l_state = load(state_hbm, state, 1)
    l_mat = load(mat_hbm, mat, 2)
    l_trim = load(trim_hbm, trim, 3)
    l_mod = load(moduli_hbm, moduli, 4)
    last = rows - 16
    l_ends = [load(basis_hbm.at[:, pl.ds(r, 16)], basis.at[:, pl.ds(r, 16)], i) for r, i in ((0, 9), (last, 10))]
    l_basis = load(basis_hbm.at[:, pl.ds(16, rows - 32)], basis.at[:, pl.ds(16, rows - 32)], 5)
    l_blk = load(blocks_hbm.at[0, 0], blk, 6)
    l_band = load(band_hbm, band, 7)
    l_inv = load(inv_hbm, inv, 8)

    def send(src, dst, ssem, rsem, to):
        copy = pltpu.make_async_remote_copy(
            src_ref=src, dst_ref=dst, send_sem=ssem, recv_sem=rsem, device_id=to, device_id_type=MESH
        )
        copy.start()
        return copy

    def tell(level):
        count = 0
        for levels, at in ((col_levels, col_at), (row_levels, row_at)):
            if level < len(levels):
                for k in levels[level]:
                    signal(entry_sem.at[level], at(k))
                count += len(levels[level])
        return count

    def hear(level, count):
        if count:
            pl.semaphore_wait(entry_sem.at[level], count)

    r16 = iota((16, cols), 0)
    c16 = iota((16, cols), 1)
    l_dir.wait()
    row_src[...] = jnp.zeros_like(row_src)
    edge_cols = jnp.zeros((16, rows), F32)
    for c in range(3):
        row_src[0, c : c + 1, :] = dpad[c, 8:9, :]
        row_src[1, c : c + 1, :] = dpad[c, 7 + rows : 8 + rows, :]
        pick = ones_where(((r16 == c) & (c16 == 0)) | ((r16 == 8 + c) & (c16 == cols - 1)))
        place[c] = pick
        edge_cols = edge_cols + mm(pick, dpad[c, 8 : 8 + rows, :].astype(BF16), NT)
    col_src[...] = edge_cols
    l_state.wait()
    l_mat.wait()
    l_trim.wait()
    l_mod.wait()
    for g in range(groups):
        at = slice(16 * g, 16 * g + 16)
        s0, s1, s2 = state[0, at, :], state[1, at, :], state[2, at, :]
        stretch = 1.0 + 0.3 * (s0 * s0 + s1 * s1 + s2 * s2)
        which = mat[at, :]
        table = jnp.full((16, cols), moduli[0], F32)
        for entry in range(1, 8):
            table = jnp.where(which == entry, moduli[entry], table)
        coef[at, :] = table * (stretch + 1.0 / stretch) * (0.25 + 0.75 * trim[at, :].astype(F32))

    for copy in l_ends:
        copy.wait()
    for i in range(2):
        edge = coef[(rows - 1) * i : (rows - 1) * i + 1, :]
        for k in range(16):
            line = basis[k, last * i : last * i + 16, :].astype(F32)[15 * i : 15 * i + 1, :]
            edge_rows[i, k : k + 1, :] = line * edge
        rim_src[i, 0:16, :] = jnp.concatenate([row_src[1 * i], jnp.zeros((8, cols), F32)], axis=0).astype(BF16)
        rim_src[i, 16:32, :] = edge_rows[i].astype(BF16)
    lane = iota((16, cols), 1)
    side = iota((16, cols), 0)
    zero_row = jnp.zeros((1, cols), F32)
    for c in range(3):
        dpad[c, 7:8, :] = zero_row
        dpad[c, 8 + rows : 9 + rows, :] = zero_row
        for g in range(groups):
            r0 = 8 + 16 * g
            at = slice(16 * g, 16 * g + 16)
            centre = dpad[c, r0 : r0 + 16, :]
            beside = dpad[c, r0 - 1 : r0 + 15, :] + dpad[c, r0 + 1 : r0 + 17, :]
            beside = beside + jnp.where(lane == 0, 0.0, pltpu.roll(centre, 1, 1))
            beside = beside + jnp.where(lane == cols - 1, 0.0, pltpu.roll(centre, cols - 1, 1))
            coupled = dpad[(c + 1) % 3, r0 : r0 + 16, :]
            value = coef[at, :] * (5.0 * centre - beside + 0.5 * coupled)
            own[c, at, :] = value
            inner[c, at, :] = value.astype(BF16)

    coef_high = coef[...].astype(BF16)
    coef_low = (coef[...] - coef_high.astype(F32)).astype(BF16)
    both = ones_where(((r16 < 8) & (c16 == 0)) | ((r16 >= 8) & (c16 == cols - 1)))
    coef_cols = mm(both, coef_high, NT) + mm(both, coef_low, NT)

    pl.semaphore_wait(barrier, len(row_first) + len(col_first))
    told = tell(0)
    halo = [
        send(col_src.at[pl.ds(0, 8)], col_dst.at[pl.ds(8, 8)], halo_ssem.at[2], halo_rsem.at[2], left),
        send(col_src.at[pl.ds(8, 8)], col_dst.at[pl.ds(0, 8)], halo_ssem.at[3], halo_rsem.at[3], right),
    ]

    @pl.when(x != 0)
    def _():
        rim_dst[0] = rim_src[0]

    rim_up = pltpu.make_async_remote_copy(
        src_ref=rim_src.at[0], dst_ref=rim_dst.at[0], send_sem=rim_ssem.at[0], recv_sem=rim_rsem.at[0],
        device_id=row_at((0, ys - 1)), device_id_type=MESH,
    )

    @pl.when(x == 0)
    def _():
        rim_up.start()

    rim_right = send(rim_src.at[1], rim_dst.at[1], rim_ssem.at[1], rim_rsem.at[1], row_at((1, 0)))

    l_basis.wait()
    r48 = iota((48, cols), 0)
    c48 = iota((48, cols), 1)
    same = (r48 % 16) == (c48 % 16)
    re = iota((cols, 128), 0)
    ce = iota((cols, 128), 1)
    fold = ones_where(((ce % 16) == (re // 16)) & (ce < 96))
    rp = iota((48, 128), 0)
    cp = iota((48, 128), 1)
    acc = jnp.zeros((48, cols), F32)
    for g in range(groups):
        own_rows = inner[:, 16 * g : 16 * g + 16, :].reshape(48, cols)
        functions = basis[:, 16 * g : 16 * g + 16, :].reshape(cols, cols)
        acc = acc + mm(own_rows, functions, NT)
    acc = jnp.where(same, acc, 0.0)
    high = acc.astype(BF16)
    low = (acc - high.astype(F32)).astype(BF16)
    part = mm(high, fold) + mm(low, fold)
    part = jnp.where((((cp // 16) % 3) == (rp // 16)) & (cp < 96), part, 0.0)
    sum1_src[...] = jnp.sum(part, axis=0, keepdims=True)

    rb = iota((32, cols), 0)
    cb = iota((32, cols), 1)
    edge_basis = jnp.zeros((32, rows), F32)
    for k in range(16):
        ends = ones_where(((rb == k) & (cb == 0)) | ((rb == 16 + k) & (cb == cols - 1)))
        edge_basis = edge_basis + mm(ends, basis[k], NT)
    edge_basis = edge_basis.astype(BF16)
    blank = jnp.zeros((32, rows), BF16)
    first_basis = jnp.concatenate([edge_basis[0:16, :]] * 6 + [blank], axis=0)
    last_basis = jnp.concatenate([edge_basis[16:32, :]] * 6 + [blank], axis=0)

    hear(0, told)
    told = tell(1)
    halo += [
        send(row_src.at[0], row_dst.at[1], halo_ssem.at[0], halo_rsem.at[0], up),
        send(row_src.at[1], row_dst.at[0], halo_ssem.at[1], halo_rsem.at[1], down),
    ]
    tan = []
    for c in range(3):
        tan.append(
            (
                send(inner.at[c, pl.ds(0, 64)], wide.at[c, pl.ds(192, 64)], tan_ssem.at[c, 0], tan_rsem.at[c, 0], up),
                send(inner.at[c, pl.ds(64, 64)], wide.at[c, pl.ds(0, 64)], tan_ssem.at[c, 1], tan_rsem.at[c, 1], down),
            )
        )

    halo[0].wait_recv()
    halo[1].wait_recv()
    half = iota((16, rows), 0)
    keep = ((half < 8) & (e > 0)) | ((half >= 8) & (e < ncol - 1))
    shares = -coef_cols * jnp.where(keep, col_dst[...], 0.0)
    shares_low = shares.astype(BF16)
    rh = iota((16, 128), 0)
    ch = iota((16, 128), 1)

    for i in range(2):
        fix_src[i, 0:16, :] = shares
        edge = coef[(rows - 1) * i : (rows - 1) * i + 1, :]
        fix_src[i, 16:24, :] = jnp.concatenate(
            [jnp.broadcast_to(edge[:, 0:128], (4, 128)), jnp.broadcast_to(edge[:, 128:256], (4, 128))], axis=0
        )
    fix = [
        send(fix_src.at[0], fix_dst.at[1], fix_ssem.at[0], fix_rsem.at[0], up),
        send(fix_src.at[1], fix_dst.at[0], fix_ssem.at[1], fix_rsem.at[1], down),
    ]

    @pl.when(x == 0)
    def _():
        rim_up.wait_recv()

    rim_right.wait_recv()
    upper = rim_dst[1]
    lower = rim_dst[0]
    values = jnp.concatenate([upper[0:16, :], lower[0:16, :]], axis=1)
    edge = jnp.concatenate([lower[16:32, :], upper[16:32, :]], axis=1)
    edge = jnp.concatenate([edge] * 6 + [jnp.zeros((32, 2 * cols), BF16)], axis=0)
    inside = (x > 0) | (y < ys - 1)
    across = jnp.where(inside, mm(values, edge, NT), 0.0)
    part = jnp.where(rh < 8, mm(shares_low, first_basis, NT) - across, mm(shares_low, last_basis, NT))
    part = jnp.where(((ch // 16) % 3 == rh % 8) & (rh % 8 < 3) & (ch < 96), part, 0.0)
    sum1_src[...] = sum1_src[...] + jnp.sum(part, axis=0, keepdims=True)
    for k in sorted(range(1, ncol), key=lambda k: (-ring(k, ncol), k)):
        send(sum1_src, sum1_dst.at[k - 1], sum_ssem.at[0], sum_rsem.at[0], col_at(k))
    hear(1, told)
    told = tell(2)

    l_blk.wait()
    l_band.wait()
    width = band[0, 0]
    for i in range(8):
        t = iota((32, 256), 0) + 32 * i
        s = iota((32, 256), 1)
        keep = jnp.abs(t - s) <= width
        keep = keep & ((s >= 64) | (d > 0)) & ((s < 192) | (d < nrow - 1))
        keep = keep & ((t >= 64) | (d > 0)) & ((t < 192) | (d < nrow - 1))
        factor = 0.5 if (i < 2 or i >= 6) else 1.0
        factor = jnp.where(keep, factor, 0.0).astype(BF16)
        for c in range(3):
            blk[c, 32 * i : 32 * i + 32, :] = blk[c, 32 * i : 32 * i + 32, :] * factor

    l_inv.wait()
    inv_high = inv[...].astype(BF16)
    inv_low = (inv[...] - inv_high.astype(F32)).astype(BF16)
    repeat = ones_where((iota((48, 768), 1) // 16) == iota((48, 768), 0))
    irep[0:48, :] = mm(inv_high, repeat, TN).astype(BF16)
    irep[48:96, :] = mm(inv_low, repeat, TN).astype(BF16)
    irep[96:128, :] = jnp.zeros((32, 768), BF16)

    halo[2].wait_recv()
    halo[3].wait_recv()
    above = jnp.where(d > 0, row_dst[0], 0.0) * -coef[0:1, :]
    below = jnp.where(d < nrow - 1, row_dst[1], 0.0) * -coef[rows - 1 : rows, :]
    for c in range(3):
        sides = mm(shares_low, place[c], TN)
        for g in range(groups):
            at = slice(16 * g, 16 * g + 16)
            value = own[c, at, :] + sides[at, :]
            if g == 0:
                value = value + jnp.where(side == 0, above[c : c + 1, :], 0.0)
            if g == groups - 1:
                value = value + jnp.where(side == 15, below[c : c + 1, :], 0.0)
            wide[c, 64 + 16 * g : 80 + 16 * g, :] = value.astype(BF16)

    def whole(buf, stage):
        return pltpu.make_async_remote_copy(
            src_ref=buf, dst_ref=buf, send_sem=sum_ssem.at[stage], recv_sem=sum_rsem.at[stage],
            device_id=right, device_id_type=MESH,
        )

    res = []

    def local(c):
        for copy in tan[c]:
            copy.wait_recv()
        if c == 0:
            for copy in fix:
                copy.wait_recv()
        for i in range(2):
            sides = mm(fix_dst[i, 0:16, :].astype(BF16), place[c], TN)
            edge = jnp.concatenate([fix_dst[i, 16:17, :], fix_dst[i, 20:21, :]], axis=1)
            beyond = dpad[c, 8:9, :] if i == 0 else dpad[c, 7 + rows : 8 + rows, :]
            for j in range(4):
                to = slice(192 * i + 16 * j, 192 * i + 16 * j + 16)
                lines = slice(64 * (1 - i) + 16 * j, 64 * (1 - i) + 16 * j + 16)
                value = wide[c, to, :].astype(F32) + sides[lines, :]
                if j == (3 if i == 0 else 0):
                    value = value - jnp.where(side == (15 if i == 0 else 0), edge * beyond, 0.0)
                wide[c, to, :] = value.astype(BF16)
        vec = wide[c]
        margins = mm(jnp.concatenate([blk[c, 0:64, :], blk[c, 192:256, :]], axis=0), vec)
        res_src[0, c] = margins[0:64, :].astype(BF16)
        res_src[1, c] = margins[64:128, :].astype(BF16)
        res.append(
            (
                send(res_src.at[0, c], res_dst.at[1, c], res_ssem.at[c, 0], res_rsem.at[c, 0], up),
                send(res_src.at[1, c], res_dst.at[0, c], res_ssem.at[c, 1], res_rsem.at[c, 1], down),
            )
        )


    whole(sum1_dst, 0).wait_recv()
    sum2_src[...] = sum1_src[...] + jnp.sum(sum1_dst[...], axis=0)
    hear(2, told)
    for offset in reversed(near_set(xs, ys, nrow)):
        slot = offset[1] * xs + offset[0] - 1
        send(sum2_src, sum2_dst.at[slot], sum_ssem.at[1], sum_rsem.at[1], row_at(offset))

    local(0)
    local(1)
    local(2)

    for c in range(3):
        own[c] = mm(blk[c, 64:192, :], wide[c])
    for c in range(3):
        for copy in res[c]:
            copy.wait_recv()
        own[c, 0:64, :] = own[c, 0:64, :] + res_dst[0, c].astype(F32)
        own[c, 64:128, :] = own[c, 64:128, :] + res_dst[1, c].astype(F32)

    for copy in halo + fix + [rim_right]:
        copy.wait_send()

    @pl.when(x == 0)
    def _():
        rim_up.wait_send()

    for c in range(3):
        for copy in tan[c] + res[c]:
            copy.wait_send()
    whole(sum1_dst, 0).wait_send()

    whole(sum2_dst, 1).wait_recv()
    total = sum2_src[...] + jnp.sum(sum2_dst[...], axis=0)
    total = jnp.broadcast_to(total, (16, 128))
    high = total.astype(BF16).astype(F32)
    mid = (total - high).astype(BF16).astype(F32)
    low = total - high - mid
    step = mm(jnp.concatenate([high, mid, low], axis=0).astype(BF16), irep[...])
    step = (step[0:16, :] + step[16:32, :] + step[32:48, :]).astype(BF16).astype(F32)
    spread = jnp.concatenate([step[:, c * cols : c * cols + cols] for c in range(3)], axis=0)
    spread = jnp.where(same, spread, 0.0).astype(BF16)
    for g in range(groups):
        at = slice(16 * g, 16 * g + 16)
        term = mm(spread, basis[:, at, :].reshape(cols, cols))
        for c in range(3):
            out[c, at, :] = own[c, at, :] + term[16 * c : 16 * c + 16, :]
    whole(sum2_dst, 1).wait_send()


def body(nrow, ncol, *args):
    vm = pltpu.VMEM
    dma = pltpu.SemaphoreType.DMA
    return pl.pallas_call(
        functools.partial(kernel, nrow, ncol),
        out_shape=vm((3, 128, 256), F32),
        in_specs=[pl.BlockSpec(memory_space=pltpu.HBM)] * 9,
        out_specs=pl.BlockSpec(memory_space=vm),
        scratch_shapes=[
            vm((3, 144, 256), F32),
            vm((3, 128, 256), F32),
            vm((128, 256), jnp.int32),
            vm((128, 256), jnp.int32),
            pltpu.SMEM((8,), F32),
            pltpu.SMEM((1, 1), jnp.int32),
            vm((3, 256, 256), BF16),
            vm((16, 128, 256), BF16),
            vm((48, 48), F32),
            vm((128, 256), F32),
            vm((3, 256, 256), BF16),
            vm((3, 128, 256), F32),
            vm((2, 8, 256), F32),
            vm((2, 8, 256), F32),
            vm((16, 128), F32),
            vm((16, 128), F32),
            vm((2, 3, 64, 256), BF16),
            vm((2, 3, 64, 256), BF16),
            vm((1, 128), F32),
            vm((ncol - 1, 1, 128), F32),
            vm((1, 128), F32),
            vm((nrow - 1, 1, 128), F32),
            vm((128, 768), BF16),
            vm((3, 16, 256), BF16),
            vm((3, 128, 256), BF16),
            vm((2, 24, 128), F32),
            vm((2, 24, 128), F32),
            vm((2, 16, 256), F32),
            vm((2, 32, 256), BF16),
            vm((2, 32, 256), BF16),
            dma((11,)),
            dma((4,)),
            dma((4,)),
            dma((3, 2)),
            dma((3, 2)),
            dma((2,)),
            dma((2,)),
            dma((2,)),
            dma((2,)),
            dma((3, 2)),
            dma((3, 2)),
            dma((2,)),
            dma((2,)),
            pltpu.SemaphoreType.REGULAR((3,)),
        ],
        compiler_params=pltpu.CompilerParams(
            collective_id=0, has_side_effects=True, vmem_limit_bytes=56 * 1024 * 1024
        ),
        name="schwarz",
    )(*args)


def solution(mesh):
    placed = (
        P(None, "prow", "pcol"),
        P(None, "prow", "pcol"),
        P("prow", "pcol"),
        P("prow", "pcol"),
        P(),
        P("prow", "pcol"),
        P("prow", "pcol", None, None, None),
        P(None, "prow", "pcol"),
        P(),
    )
    return jax.shard_map(
        functools.partial(body, mesh.shape["prow"], mesh.shape["pcol"]),
        mesh=mesh,
        in_specs=placed,
        out_specs=P(None, "prow", "pcol"),
        check_vma=False,
    )
```
